128 devices in a mesh: pipe: 16 (over z, y_lo, core), tensor: 8 (over x, y_hi).
Axes of the slice: x: 4, y: 4 (y_hi: 2, y_lo: 2; y = y_hi * 2 + y_lo), z: 4, core: 2. Of those that a mesh axis runs over, the one named last changes fastest.
Arguments:
- tokens: bfloat16 [1024, 8192], P('tensor', 'pipe'), may hold values from -6 to 6
- gate_weight: bfloat16 [8192, 28672], P('pipe', 'tensor'), may hold values from -0.0625 to 0.0625
- up_weight: bfloat16 [8192, 28672], P('pipe', 'tensor'), may hold values from -0.0625 to 0.0625
- down_weight: bfloat16 [28672, 8192], P('tensor', 'pipe'), may hold values from -0.03125 to 0.03125
- out_grad: bfloat16 [1024, 8192], P('tensor', 'pipe'), may hold values from -6 to 6
Outputs:
- output: bfloat16 [1024, 8192], P('tensor', 'pipe')
- input_grad: bfloat16 [1024, 8192], P('tensor', 'pipe')
- gate_grad: bfloat16 [8192, 28672], P('pipe', 'tensor')
- up_grad: bfloat16 [8192, 28672], P('pipe', 'tensor')
- down_grad: bfloat16 [28672, 8192], P('tensor', 'pipe')
The draws below stay inside these ranges and needn't reach their ends.
All inputs are finite; a program needn't handle non-finite values.
Results may differ from the reference program's by a relative error of at most 0.005.
Values may be sent and summed in bfloat16 or wider, within the bound.
A program may use at most 256 MiB of HBM per device.

```python
import jax
import jax.numpy as jnp

D = 8192
FF = 28672
TOKENS = 1024


def block_scale(rng, shape, pieces, low, top_value):
    loudness, own = 1.0, jax.random.fold_in(rng, 6)
    for dim, parts in pieces:
        draws = jnp.exp(jax.random.uniform(jax.random.fold_in(own, dim), (parts,), jnp.float32, low / len(pieces), top_value / len(pieces)))
        loudness = loudness * jnp.repeat(draws, shape[dim] // parts).reshape([-1 if axis == dim else 1 for axis in range(len(shape))])
    return loudness


def centred(own_key, dims, width, most, split=(), dtype=jnp.bfloat16):
    array = jax.random.normal(own_key, dims, jnp.float32) * width
    if len(split) > 0:
        array = block_scale(own_key, dims, split, -0.22, 0.18) * array
    return jnp.clip(array, min=-most, max=most).astype(dtype)


def setup_inputs(seed: int = 0) -> dict:
    keys = jax.random.split(jax.random.key(seed), 6)
    return {
        "tokens": centred(keys[0], (TOKENS, D), 1.0, 6.0, ((0, 8), (1, 16))),
        "gate_weight": centred(keys[1], (D, FF), D ** -0.5, 0.0625, ((0, 16), (1, 8))),
        "up_weight": centred(keys[2], (D, FF), D ** -0.5, 0.0625, ((0, 16), (1, 8))),
        "down_weight": centred(keys[3], (FF, D), FF ** -0.5, 0.03125, ((0, 8), (1, 16))),
        "out_grad": centred(keys[4], (TOKENS, D), 1.0, 6.0, ((0, 8), (1, 16))),
    }


def reference(tokens, gate_weight, up_weight, down_weight, out_grad):
    gate_value = jnp.dot(tokens, gate_weight, preferred_element_type=jnp.float32)
    up_value = jnp.dot(tokens, up_weight, preferred_element_type=jnp.float32)
    sigma_gate = jax.nn.sigmoid(gate_value)
    swish_gate = gate_value * sigma_gate
    hidden = (swish_gate * up_value).astype(jnp.bfloat16)
    output = jnp.dot(hidden, down_weight, preferred_element_type=jnp.float32).astype(jnp.bfloat16)
    hidden_grad = jnp.dot(out_grad, down_weight.T, preferred_element_type=jnp.float32)
    gate_delta = (hidden_grad * up_value * sigma_gate * (1.0 + gate_value * (1.0 - sigma_gate))).astype(jnp.bfloat16)
    up_delta = (hidden_grad * swish_gate).astype(jnp.bfloat16)
    input_grad = (jnp.dot(gate_delta, gate_weight.T, preferred_element_type=jnp.float32) + jnp.dot(up_delta, up_weight.T, preferred_element_type=jnp.float32)).astype(jnp.bfloat16)
    gate_grad = jnp.dot(tokens.T, gate_delta, preferred_element_type=jnp.float32).astype(jnp.bfloat16)
    up_grad = jnp.dot(tokens.T, up_delta, preferred_element_type=jnp.float32).astype(jnp.bfloat16)
    down_grad = jnp.dot(hidden.T, out_grad, preferred_element_type=jnp.float32).astype(jnp.bfloat16)
    return output, input_grad, gate_grad, up_grad, down_grad
```

```python
import functools

import jax
import jax.numpy as jnp
from jax import lax
from jax.experimental import pallas as pl
from jax.experimental.pallas import tpu as pltpu
from jax.sharding import PartitionSpec as P

MESH = pl.DeviceIdType.MESH
BF = jnp.bfloat16
F32 = jnp.float32
CW = 128
SLOTS = 6
LAG_SUM = 2
LAG_USE = 4


def dot_nn(a, b):
    return lax.dot_general(a, b, (((1,), (0,)), ((), ())), preferred_element_type=F32)


def dot_nt(a, b):
    return lax.dot_general(a, b, (((1,), (1,)), ((), ())), preferred_element_type=F32)


def dot_tn(a, b):
    return lax.dot_general(a, b, (((0,), (0,)), ((), ())), preferred_element_type=F32)


def drain(ref, sem):
    pltpu.make_async_copy(ref, ref, sem).wait()


def kernel(
    dims,
    tok, wg, wu, wd, og,
    out, ig, gg, ug, dg,
    w_gu, w_d, x_all, x_t, o_all, h_all, d_all, out_acc, in_acc, part, part_h,
    s_gu, r_gu, own_gu, s_hg, r_hg, own_hg, gu, st_d, st_gu, rx, ts, tr, to,
    ld_w, rv_w, sd_w, ld_d, rv_d, sd_d, ld_a, rv_a, sd_a, rf_a, sf_a,
    sd_gu, rv_gu, sd_hg, rv_hg, sd_h, rv_h, sd_dl, rv_dl,
    l_dg, s_dg, r_dg, l_gu, s_gg, r_gg, s_x, r_x, s_t, r_t, l_o,
):
    nq, nt, td, dd, tq, fh, nc = dims
    pipe, t = lax.axis_index("pipe"), lax.axis_index("tensor")
    q, c = pipe // 2, pipe % 2
    oc = 1 - c
    tokens = nt * td

    def group(d):
        return ((q ^ d) * 2 + c, t)

    def shard(d):
        return (pipe, t ^ d)

    other = (q * 2 + oc, t)

    def send(src, dst, s, r, dev):
        pltpu.make_async_remote_copy(
            src_ref=src, dst_ref=dst, send_sem=s, recv_sem=r, device_id=dev, device_id_type=MESH
        ).start()

    def at(i, n):
        return pl.ds(pl.multiple_of(i * n, n), n)

    mine, theirs = at(c, dd), at(oc, dd)

    barrier = pltpu.get_barrier_semaphore()
    for d in range(1, nq):
        pl.semaphore_signal(barrier, inc=1, device_id=group(d), device_id_type=MESH)
    for d in range(1, nt):
        pl.semaphore_signal(barrier, inc=1, device_id=shard(d), device_id_type=MESH)
    pl.semaphore_signal(barrier, inc=1, device_id=other, device_id_type=MESH)
    pl.semaphore_wait(barrier, nq + nt - 1)

    for k, (src, dst) in enumerate(((tok, x_all), (og, o_all))):
        block = dst.at[at(t, td), mine]
        pltpu.make_async_copy(src, block, ld_a.at[k]).start()
        for d in range(1, nt):
            send(src, block, sd_a.at[k], rv_a.at[k, d], shard(d))
        send(src, block, sd_a.at[k], rf_a.at[k, 0], other)

        if k == 0:
            @pl.loop(0, nc)
            def _(i):
                keep = pl.ds(pl.multiple_of(c * fh + i * CW, CW), CW)
                give = pl.ds(pl.multiple_of(oc * fh + i * CW, CW), CW)
                for j, w in enumerate((wg, wu)):
                    place = w_gu.at[i, mine, pl.ds(j * CW, CW)]
                    pltpu.make_async_copy(w.at[:, keep], place, ld_w.at[i]).start()
                    send(w.at[:, give], place, sd_w, rv_w.at[i], other)

            pltpu.make_async_copy(wd.at[at(c, fh), :], w_d.at[:, mine], ld_d).start()
            send(wd.at[at(oc, fh), :], w_d.at[:, mine], sd_d, rv_d, other)

    def forward_blocks(k, ref):
        for d in range(1, nt):
            block = ref.at[at(t ^ d, td), mine]
            drain(block, rv_a.at[k, d])
            send(block, block, sf_a.at[k], rf_a.at[k, d], other)

    def await_blocks(k, ref):
        drain(ref.at[at(t, td), mine], ld_a.at[k])
        for d in range(nt):
            drain(ref.at[at(t ^ d, td), theirs], rf_a.at[k, d])

    forward_blocks(0, x_all)
    await_blocks(0, x_all)

    half = tokens // 2
    rows = tokens // 4

    def fwd_partial(i):
        slot = lax.rem(i, SLOTS)

        @pl.when(i >= SLOTS)
        def _():
            drain(s_gu.at[slot, pl.ds(0, (nq - 1) * tq)], sd_gu.at[slot])

        drain(w_gu.at[i, mine], ld_w.at[i])
        drain(w_gu.at[i, theirs], rv_w.at[i])

        @pl.loop(0, 2)
        def _(m):
            value = dot_nn(x_all[at(m, half), :], w_gu[i])
            part[at(m, half), :] = value
            s_gu[slot, at(m, half), :] = value.astype(BF)

        own_gu[slot] = part[at(q, tq), :]
        for d in range(1, nq):
            send(s_gu.at[slot, at(q ^ d, tq)], r_gu.at[slot, d - 1], sd_gu.at[slot], rv_gu.at[slot], group(d))

    def fwd_sum(i):
        slot = lax.rem(i, SLOTS)
        drain(r_gu.at[slot], rv_gu.at[slot])
        total = own_gu[slot]
        for d in range(nq - 1):
            total = total + r_gu[slot, d].astype(F32)
        gu[i] = total
        gate, up = total[:, :CW], total[:, CW:]
        h_all[i, at(q, tq), :] = (gate * jax.nn.sigmoid(gate) * up).astype(BF)
        block = h_all.at[i, at(q, tq)]
        for d in range(1, nq):
            send(block, block, sd_h.at[i], rv_h.at[i], group(d))

    def fwd_use(i):
        drain(h_all.at[i, pl.ds(0, (nq - 1) * tq)], rv_h.at[i])
        drain(h_all.at[i, pl.ds(0, (nq - 1) * tq)], sd_h.at[i])

        @pl.loop(0, 4)
        def _(m):
            value = dot_nn(h_all[i, at(m, rows), :], w_d[at(i, CW), :])

            @pl.when(i == 0)
            def _():
                out_acc[at(m, rows), :] = value

            @pl.when(i > 0)
            def _():
                out_acc[at(m, rows), :] += value

        s = lax.rem(i, 2)
        place = pl.ds(pl.multiple_of(c * fh + i * CW, CW), CW)

        @pl.when(i >= 2)
        def _():
            drain(st_d.at[s, :, mine], l_dg.at[s])
            drain(st_d.at[s, :, theirs], s_dg.at[s])

        st_d[s] = dot_tn(h_all[i], o_all[...]).astype(BF)
        pltpu.make_async_copy(st_d.at[s, :, mine], dg.at[place, :], l_dg.at[s]).start()
        send(st_d.at[s, :, theirs], dg.at[place, :], s_dg.at[s], r_dg, other)

    def bwd_partial(i):
        slot = lax.rem(i, SLOTS)

        @pl.when(i >= SLOTS)
        def _():
            drain(s_hg.at[slot, pl.ds(0, (nq - 1) * tq)], sd_hg.at[slot])

        @pl.loop(0, 2)
        def _(m):
            value = dot_nt(o_all[at(m, half), :], w_d[at(i, CW), :])
            part_h[at(m, half), :] = value
            s_hg[slot, at(m, half), :] = value.astype(BF)

        own_hg[slot] = part_h[at(q, tq), :]
        for d in range(1, nq):
            send(s_hg.at[slot, at(q ^ d, tq)], r_hg.at[slot, d - 1], sd_hg.at[slot], rv_hg.at[slot], group(d))

    def bwd_sum(i):
        slot = lax.rem(i, SLOTS)
        drain(r_hg.at[slot], rv_hg.at[slot])
        total = own_hg[slot]
        for d in range(nq - 1):
            total = total + r_hg[slot, d].astype(F32)
        gate, up = gu[i, :, :CW], gu[i, :, CW:]
        sigma = jax.nn.sigmoid(gate)
        d_all[i, at(q, tq), :CW] = (total * up * sigma * (1.0 + gate * (1.0 - sigma))).astype(BF)
        d_all[i, at(q, tq), CW:] = (total * (gate * sigma)).astype(BF)
        block = d_all.at[i, at(q, tq)]
        for d in range(1, nq):
            send(block, block, sd_dl.at[i], rv_dl.at[i], group(d))

    def bwd_use(i):
        drain(d_all.at[i, pl.ds(0, (nq - 1) * tq)], rv_dl.at[i])
        drain(d_all.at[i, pl.ds(0, (nq - 1) * tq)], sd_dl.at[i])
        s = lax.rem(i, 2)
        place = pl.ds(pl.multiple_of(c * fh + i * CW, CW), CW)

        @pl.when(i >= 2)
        def _():
            drain(st_gu.at[s, mine], l_gu.at[s])
            drain(st_gu.at[s, theirs], s_gg.at[s])

        @pl.loop(0, 2)
        def _(m):
            st_gu[s, at(m, dd), :] = dot_nn(x_t[at(m, dd), :], d_all[i]).astype(BF)

        for j, (grad, r) in enumerate(((gg, 0), (ug, 1))):
            lanes = pl.ds(j * CW, CW)
            pltpu.make_async_copy(st_gu.at[s, mine, lanes], grad.at[:, place], l_gu.at[s]).start()
            send(st_gu.at[s, theirs, lanes], grad.at[:, place], s_gg.at[s], r_gg.at[r], other)

        @pl.loop(0, 4)
        def _(m):
            value = dot_nt(d_all[i, at(m, rows), :], w_gu[i])

            @pl.when(i == 0)
            def _():
                in_acc[at(m, rows), :] = value

            @pl.when(i > 0)
            def _():
                in_acc[at(m, rows), :] += value

    def reduce_pair(k, acc):
        send(acc.at[:, theirs], rx.at[k], s_x.at[k], r_x.at[k], other)

    def reduce_send(k, acc):
        drain(rx.at[k], r_x.at[k])

        @pl.loop(0, nt)
        def _(j):
            value = acc[at(j, td), mine] + rx[k, at(j, td), :]
            rx[k, at(j, td), :] = value
            ts[k, at(j, td), :] = value.astype(BF)

        for d in range(1, nt):
            send(ts.at[k, at(t ^ d, td)], tr.at[k, d - 1], s_t.at[k], r_t.at[k], shard(d))

    def reduce_done(k, result):
        drain(tr.at[k], r_t.at[k])
        total = rx[k, at(t, td), :]
        for d in range(nt - 1):
            total = total + tr[k, d].astype(F32)
        to[k] = total.astype(BF)
        pltpu.make_async_copy(to.at[k], result, l_o.at[k]).start()
        drain(rx.at[k], s_x.at[k])
        drain(ts.at[k, pl.ds(0, (nt - 1) * td)], s_t.at[k])

    steps = 2 * nc + LAG_USE

    @pl.loop(0, steps)
    def _(v):
        @pl.when(v < nc)
        def _():
            fwd_partial(v)

        @pl.when((v >= nc) & (v < 2 * nc))
        def _():
            bwd_partial(v - nc)

        @pl.when(v == LAG_USE - 1)
        def _():
            forward_blocks(1, o_all)
            drain(w_d.at[:, mine], ld_d)
            drain(w_d.at[:, theirs], rv_d)

            @pl.loop(0, nt)
            def _(j):
                x_t[:, at(j, td)] = x_all[at(j, td), :].T

        @pl.when((v >= LAG_SUM) & (v < nc + LAG_SUM))
        def _():
            fwd_sum(v - LAG_SUM)

        @pl.when((v >= nc + LAG_SUM) & (v < 2 * nc + LAG_SUM))
        def _():
            bwd_sum(v - nc - LAG_SUM)

        @pl.when(v == LAG_USE)
        def _():
            await_blocks(1, o_all)

        @pl.when((v >= LAG_USE) & (v < nc + LAG_USE))
        def _():
            fwd_use(v - LAG_USE)

        @pl.when(v >= nc + LAG_USE)
        def _():
            bwd_use(v - nc - LAG_USE)

        @pl.when(v == nc + LAG_USE)
        def _():
            reduce_pair(0, out_acc)

        @pl.when(v == nc + LAG_USE + 1)
        def _():
            reduce_send(0, out_acc)

        @pl.when(v == nc + LAG_USE + 5)
        def _():
            reduce_done(0, out)

    reduce_pair(1, in_acc)
    reduce_send(1, in_acc)
    reduce_done(1, ig)

    for s in range(SLOTS):
        drain(s_gu.at[s, pl.ds(0, (nq - 1) * tq)], sd_gu.at[s])
        drain(s_hg.at[s, pl.ds(0, (nq - 1) * tq)], sd_hg.at[s])
    for s in range(2):
        drain(st_d.at[s, :, mine], l_dg.at[s])
        drain(st_d.at[s, :, theirs], s_dg.at[s])
        drain(st_gu.at[s, mine], l_gu.at[s])
        drain(st_gu.at[s, theirs], s_gg.at[s])
        drain(to.at[s], l_o.at[s])
    partner = at(oc, fh)
    drain(dg.at[partner, :], r_dg)
    drain(gg.at[:, partner], r_gg.at[0])
    drain(ug.at[:, partner], r_gg.at[1])
    drain(w_gu.at[:, mine], sd_w)
    drain(w_d.at[:, mine], sd_d)
    for k, ref in enumerate((x_all, o_all)):
        drain(ref.at[:, pl.ds(0, dd)], sd_a.at[k])
        drain(ref.at[pl.ds(0, (nt - 1) * td), pl.ds(0, dd)], sf_a.at[k])


def per_device(tokens, gate_weight, up_weight, down_weight, out_grad):
    nq, nt = lax.axis_size("pipe") // 2, lax.axis_size("tensor")
    td, dd = tokens.shape
    ff = gate_weight.shape[1]
    fh = ff // 2
    nc = fh // CW
    n = nt * td
    tq = n // nq
    d2 = 2 * dd
    vmem = pltpu.VMEM
    dma = pltpu.SemaphoreType.DMA
    anywhere = pl.BlockSpec(memory_space=pl.ANY)
    return pl.pallas_call(
        functools.partial(kernel, (nq, nt, td, dd, tq, fh, nc)),
        name="swiglu",
        out_shape=(
            jax.ShapeDtypeStruct((td, dd), BF),
            jax.ShapeDtypeStruct((td, dd), BF),
            jax.ShapeDtypeStruct((dd, ff), BF),
            jax.ShapeDtypeStruct((dd, ff), BF),
            jax.ShapeDtypeStruct((ff, dd), BF),
        ),
        in_specs=[anywhere] * 5,
        out_specs=(anywhere,) * 5,
        scratch_shapes=[
            vmem((nc, d2, 2 * CW), BF),
            vmem((fh, d2), BF),
            vmem((n, d2), BF),
            vmem((d2, n), BF),
            vmem((n, d2), BF),
            vmem((nc, n, CW), BF),
            vmem((nc, n, 2 * CW), BF),
            vmem((n, d2), F32),
            vmem((n, d2), F32),
            vmem((n, 2 * CW), F32),
            vmem((n, CW), F32),
            vmem((SLOTS, n, 2 * CW), BF),
            vmem((SLOTS, nq - 1, tq, 2 * CW), BF),
            vmem((SLOTS, tq, 2 * CW), F32),
            vmem((SLOTS, n, CW), BF),
            vmem((SLOTS, nq - 1, tq, CW), BF),
            vmem((SLOTS, tq, CW), F32),
            vmem((nc, tq, 2 * CW), F32),
            vmem((2, CW, d2), BF),
            vmem((2, d2, 2 * CW), BF),
            vmem((2, n, dd), F32),
            vmem((2, n, dd), BF),
            vmem((2, nt - 1, td, dd), BF),
            vmem((2, td, dd), BF),
            dma((nc,)), dma((nc,)), dma,
            dma, dma, dma,
            dma((2,)), dma((2, nt)), dma((2,)), dma((2, nt)), dma((2,)),
            dma((SLOTS,)), dma((SLOTS,)), dma((SLOTS,)), dma((SLOTS,)),
            dma((nc,)), dma((nc,)), dma((nc,)), dma((nc,)),
            dma((2,)), dma((2,)), dma,
            dma((2,)), dma((2,)), dma((2,)),
            dma((2,)), dma((2,)), dma((2,)), dma((2,)), dma((2,)),
        ],
        compiler_params=pltpu.CompilerParams(
            collective_id=0, has_side_effects=True, vmem_limit_bytes=63 * 1024 * 1024
        ),
        cost_estimate=pl.CostEstimate(flops=18 * n * d2 * fh, bytes_accessed=6 * ff * dd * 2, transcendentals=0),
    )(tokens, gate_weight, up_weight, down_weight, out_grad)


def solution(mesh):
    act, wide, tall = P("tensor", "pipe"), P("pipe", "tensor"), P("tensor", "pipe")
    return jax.shard_map(
        per_device,
        mesh=mesh,
        in_specs=(act, wide, wide, tall, act),
        out_specs=(act, act, wide, wide, tall),
        check_vma=False,
    )
```

```python
import functools

import jax
import jax.numpy as jnp
from jax import lax
from jax.experimental import pallas as pl
from jax.experimental.pallas import tpu as pltpu
from jax.sharding import PartitionSpec as P

MESH = pl.DeviceIdType.MESH
BF = jnp.bfloat16
F32 = jnp.float32
NZ = 4
CW = 128
SLOTS = 8
LAG = (2, 4, 6, 8, 10, 12)


def dot_nn(a, b):
    return lax.dot_general(a, b, (((1,), (0,)), ((), ())), preferred_element_type=F32)


def dot_nt(a, b):
    return lax.dot_general(a, b, (((1,), (1,)), ((), ())), preferred_element_type=F32)


def dot_tn(a, b):
    return lax.dot_general(a, b, (((0,), (0,)), ((), ())), preferred_element_type=F32)


def drain(ref, sem):
    pltpu.make_async_copy(ref, ref, sem).wait()


def kernel(
    dims,
    tok, wg, wu, wd, og,
    out, ig, gg, ug, dg,
    w_gu, w_d, x_all, x_t, o_all, h_all, d_all, out_acc, in_acc, part,
    keep, s1, s2, s3, r1, r2, r3, gu, st_d, st_gu, rx, ry, ta, ra, tb, rb, tc, rc, to,
    ld_w, rv_w, sd_w, ld_d, rv_d, sd_d, ld_a, rv_a, sd_a, rf_a, sf_a,
    sd_1, sd_2, sd_3, rv_1, rv_2, rv_3, rv_4, sd_h, rv_h, sd_dl, rv_dl,
    l_dg, s_dg, r_dg, l_gu, s_gg, r_gg, s_x, r_x, s_a, r_a, s_b, r_b, s_c, r_c, s_y, r_y, l_o,
):
    nt, td, dd, tq, fh, nc = dims
    pipe, t = lax.axis_index("pipe"), lax.axis_index("tensor")
    q, c = pipe // 2, pipe % 2
    oc = 1 - c
    tokens = nt * td

    z, y = q // 2, q % 2

    def chip(dz, dy):
        return lax.rem(z + dz + NZ, NZ) * 2 + (y ^ dy)

    up_z, down_z, over_y = ((chip(dz, dy) * 2 + c, t) for dz, dy in ((1, 0), (-1, 0), (0, 1)))

    def shard(d):
        return (pipe, t ^ d)

    other = (q * 2 + oc, t)

    def send(src, dst, s, r, dev):
        pltpu.make_async_remote_copy(
            src_ref=src, dst_ref=dst, send_sem=s, recv_sem=r, device_id=dev, device_id_type=MESH
        ).start()

    def at(i, n):
        return pl.ds(pl.multiple_of(i * n, n), n)

    mine, theirs = at(c, dd), at(oc, dd)

    barrier = pltpu.get_barrier_semaphore()
    for near in (up_z, down_z, over_y):
        pl.semaphore_signal(barrier, inc=1, device_id=near, device_id_type=MESH)
    for d in (1, 2, 4, 6):
        pl.semaphore_signal(barrier, inc=1, device_id=shard(d), device_id_type=MESH)
    pl.semaphore_signal(barrier, inc=1, device_id=other, device_id_type=MESH)
    pl.semaphore_wait(barrier, 8)

    def spread(k, src, dst):
        block = dst.at[at(t, td), mine]
        pltpu.make_async_copy(src, block, ld_a.at[k]).start()
        for d in (1, 2, 4, 6):
            send(src, block, sd_a.at[k], rv_a.at[k, d], shard(d))
        send(src, block, sd_a.at[k], rf_a.at[k, 0], other)

    spread(0, tok, x_all)

    @pl.loop(0, nc)
    def _(i):
        keep_cols = pl.ds(pl.multiple_of(c * fh + i * CW, CW), CW)
        give_cols = pl.ds(pl.multiple_of(oc * fh + i * CW, CW), CW)
        for j, w in enumerate((wg, wu)):
            place = w_gu.at[i, mine, pl.ds(j * CW, CW)]
            pltpu.make_async_copy(w.at[:, keep_cols], place, ld_w.at[i]).start()
            send(w.at[:, give_cols], place, sd_w, rv_w.at[i], other)

    pltpu.make_async_copy(wd.at[at(c, fh), :], w_d.at[:, mine], ld_d).start()
    send(wd.at[at(oc, fh), :], w_d.at[:, mine], sd_d, rv_d, other)

    hd = dd // 2

    def forward_blocks(k, ref):
        left = pl.ds(pl.multiple_of(c * dd, hd), hd)
        right = pl.ds(pl.multiple_of(c * dd + hd, hd), hd)
        for d in (1, 2, 4, 6, 3, 5, 7):
            place = at(t ^ d, td)
            block = ref.at[place, mine]
            drain(block, rv_a.at[k, d])
            if d == 1:
                for e in (2, 4, 6):
                    part_block = ref.at[place, left]
                    send(part_block, part_block, sd_a.at[k], rv_a.at[k, e + 1], shard(e))
            elif d % 2 == 0:
                part_block = ref.at[place, right]
                send(part_block, part_block, sd_a.at[k], rv_a.at[k, d + 1], shard(1))
            send(block, block, sf_a.at[k], rf_a.at[k, d], other)

    def await_blocks(k, ref):
        drain(ref.at[at(t, td), mine], ld_a.at[k])
        for d in range(nt):
            drain(ref.at[at(t ^ d, td), theirs], rf_a.at[k, d])

    forward_blocks(0, x_all)
    spread(1, og, o_all)
    await_blocks(0, x_all)

    half = tokens // 2

    hq = tq // 2
    low, high = pl.ds(0, hq), pl.ds(hq, hq)

    def sum_first(v, width):
        slot, w = lax.rem(v, SLOTS), pl.ds(0, width)
        for j, (dz, dy) in enumerate(((0, 0), (1, 0), (-1, 0), (2, 0), (0, 1))):
            keep[slot, j, :, w] = part[at(chip(dz, dy), tq), w]
        for j, (dz, dev) in enumerate(((2, over_y), (1, up_z), (-1, down_z))):
            s1[slot, j, :, w] = part[at(chip(dz, 1), tq), w].astype(BF)
            send(s1.at[slot, j, :, w], r1.at[slot, j, :, w], sd_1.at[slot], rv_1.at[slot], dev)

    def sum_second(v, width):
        slot, w = lax.rem(v, SLOTS), pl.ds(0, width)
        drain(r1.at[slot, :, :, w], rv_1.at[slot])
        s2[slot, 0, :, w] = (keep[slot, 3, :, w] + r1[slot, 0, :, w].astype(F32)).astype(BF)
        s2[slot, 1, :, w] = (
            keep[slot, 4, :, w] + r1[slot, 1, :, w].astype(F32) + r1[slot, 2, :, w].astype(F32)
        ).astype(BF)
        for rows, dev in ((low, down_z), (high, up_z)):
            send(s2.at[slot, 0, rows, w], r2.at[slot, 0, rows, w], sd_2.at[slot], rv_2.at[slot], dev)
        send(s2.at[slot, 1, :, w], r2.at[slot, 1, :, w], sd_2.at[slot], rv_3.at[slot], over_y)

    def sum_third(v, width):
        slot, w = lax.rem(v, SLOTS), pl.ds(0, width)
        drain(r2.at[slot, 0, :, w], rv_2.at[slot])
        s3[slot, 0, low, w] = (keep[slot, 2, low, w] + r2[slot, 0, low, w].astype(F32)).astype(BF)
        s3[slot, 0, high, w] = keep[slot, 2, high, w].astype(BF)
        s3[slot, 1, low, w] = keep[slot, 1, low, w].astype(BF)
        s3[slot, 1, high, w] = (keep[slot, 1, high, w] + r2[slot, 0, high, w].astype(F32)).astype(BF)
        for j, dev in enumerate((down_z, up_z)):
            send(s3.at[slot, j, :, w], r3.at[slot, j, :, w], sd_3.at[slot], rv_4.at[slot], dev)

    def sum_total(v, width):
        slot, w = lax.rem(v, SLOTS), pl.ds(0, width)
        drain(r2.at[slot, 1, :, w], rv_3.at[slot])
        drain(r3.at[slot, :, :, w], rv_4.at[slot])
        return (
            (keep[slot, 0, :, w] + r2[slot, 1, :, w].astype(F32))
            + (r3[slot, 0, :, w].astype(F32) + r3[slot, 1, :, w].astype(F32))
        )

    def sum_sent(v, width):
        slot, w = lax.rem(v, SLOTS), pl.ds(0, width)
        drain(s1.at[slot, :, :, w], sd_1.at[slot])
        drain(s2.at[slot, :, :, w], sd_2.at[slot])
        drain(s3.at[slot, :, :, w], sd_3.at[slot])

    def gather_first(ref, sd, rv):
        block = ref.at[at(q, tq)]
        for dev in (up_z, down_z, over_y):
            send(block, block, sd, rv.at[0], dev)

    def gather_second(ref, sd, rv, crossings):
        drain(ref.at[pl.ds(0, 3 * tq)], rv.at[0])
        below, above, beside = (chip(dz, dy) * tq for dz, dy in ((-1, 0), (1, 0), (0, 1)))
        moves = [(below, hq, up_z), (above + hq, hq, down_z)]
        if crossings == 3:
            moves += [(below, tq, over_y), (above, tq, over_y)]
        else:
            moves += [(beside, tq, up_z), (beside, tq, down_z)]
        for first, n, dev in moves:
            block = ref.at[pl.ds(pl.multiple_of(first, hq), n)]
            send(block, block, sd, rv.at[1], dev)

    def gather_third(ref, sd, rv, crossings):
        drain(ref.at[pl.ds(0, 3 * tq)], rv.at[1])
        if crossings == 3:
            moves = [(chip(-1, 1) * tq, hq, up_z), (chip(1, 1) * tq + hq, hq, down_z)]
        else:
            moves = [(chip(2, 0) * tq, tq, over_y)]
        for first, n, dev in moves:
            block = ref.at[pl.ds(pl.multiple_of(first, hq), n)]
            send(block, block, sd, rv.at[2], dev)

    def gather_done(ref, sd, rv):
        drain(ref.at[pl.ds(0, tq)], rv.at[2])
        drain(ref.at[pl.ds(0, 7 * tq)], sd)

    def fwd_partial(v):
        drain(w_gu.at[v, mine], ld_w.at[v])
        drain(w_gu.at[v, theirs], rv_w.at[v])

        @pl.loop(0, 2)
        def _(m):
            part[at(m, half), :] = dot_nn(x_all[at(m, half), :], w_gu[v])

        sum_first(v, 2 * CW)

    def fwd_sum(v):
        total = sum_total(v, 2 * CW)
        gu[v] = total
        gate, up = total[:, :CW], total[:, CW:]
        h_all[v, at(q, tq), :] = (gate * jax.nn.sigmoid(gate) * up).astype(BF)
        gather_first(h_all.at[v], sd_h.at[v], rv_h.at[v])

    def fwd_use(i):
        gather_done(h_all.at[i], sd_h.at[i], rv_h.at[i])

        @pl.loop(0, 4)
        def _(m):
            cols = pl.ds(pl.multiple_of(((oc * 2 + m) % 4) * hd, hd), hd)
            value = dot_nn(h_all[i], w_d[at(i, CW), cols])

            @pl.when(i == 0)
            def _():
                out_acc[:, cols] = value

            @pl.when(i > 0)
            def _():
                out_acc[:, cols] += value

            @pl.when((i == nc - 1) & (m < 2))
            def _():
                send(out_acc.at[:, cols], rx.at[0, m], s_x.at[0], r_x.at[0, m], other)

        s = lax.rem(i, 2)
        place = pl.ds(pl.multiple_of(c * fh + i * CW, CW), CW)

        @pl.when(i >= 2)
        def _():
            drain(st_d.at[s, :, mine], l_dg.at[s])
            drain(st_d.at[s, :, theirs], s_dg.at[s])

        st_d[s] = dot_tn(h_all[i], o_all[...]).astype(BF)
        pltpu.make_async_copy(st_d.at[s, :, mine], dg.at[place, :], l_dg.at[s]).start()
        send(st_d.at[s, :, theirs], dg.at[place, :], s_dg.at[s], r_dg, other)

    def bwd_partial(v):
        @pl.loop(0, 2)
        def _(m):
            part[at(m, half), pl.ds(0, CW)] = dot_nt(o_all[at(m, half), :], w_d[at(v - nc, CW), :])

        sum_first(v, CW)

    def bwd_sum(v):
        total = sum_total(v, CW)
        i = v - nc
        gate, up = gu[i, :, :CW], gu[i, :, CW:]
        sigma = jax.nn.sigmoid(gate)
        d_all[i, at(q, tq), :CW] = (total * up * sigma * (1.0 + gate * (1.0 - sigma))).astype(BF)
        d_all[i, at(q, tq), CW:] = (total * (gate * sigma)).astype(BF)
        gather_first(d_all.at[i], sd_dl.at[i], rv_dl.at[i])

    def bwd_use(i):
        gather_done(d_all.at[i], sd_dl.at[i], rv_dl.at[i])

        @pl.loop(0, 4)
        def _(m):
            cols = pl.ds(pl.multiple_of(((oc * 2 + m) % 4) * hd, hd), hd)
            value = dot_nt(d_all[i], w_gu[i, pl.ds(pl.multiple_of(((oc * 2 + m) % 4) * hd, hd), hd), :])

            @pl.when(i == 0)
            def _():
                in_acc[:, cols] = value

            @pl.when(i > 0)
            def _():
                in_acc[:, cols] += value

            @pl.when((i == nc - 1) & (m < 2))
            def _():
                send(in_acc.at[:, cols], rx.at[1, m], s_x.at[1], r_x.at[1, m], other)

        s = lax.rem(i, 2)
        place = pl.ds(pl.multiple_of(c * fh + i * CW, CW), CW)

        @pl.when(i >= 2)
        def _():
            drain(st_gu.at[s, mine], l_gu.at[s])
            drain(st_gu.at[s, theirs], s_gg.at[s])

        @pl.loop(0, 2)
        def _(m):
            st_gu[s, at(m, dd), :] = dot_nn(x_t[at(m, dd), :], d_all[i]).astype(BF)

        for j, (grad, r) in enumerate(((gg, 0), (ug, 1))):
            lanes = pl.ds(j * CW, CW)
            pltpu.make_async_copy(st_gu.at[s, mine, lanes], grad.at[:, place], l_gu.at[s]).start()
            send(st_gu.at[s, theirs, lanes], grad.at[:, place], s_gg.at[s], r_gg.at[r], other)

    x, h = t // 2, t % 2
    left = pl.ds(pl.multiple_of(c * dd, hd), hd)
    right = pl.ds(pl.multiple_of(c * dd + hd, hd), hd)

    def reduce_left(k, acc):
        drain(rx.at[k, 0], r_x.at[k, 0])
        for m in range(4):
            strip = at(x ^ ((m + 1) % 4), 2 * td)
            value = acc[strip, left] + rx[k, 0, strip, :]
            if m < 3:
                ta[k, m] = value.astype(BF)
                send(ta.at[k, m], ra.at[k, m], s_a.at[k], r_a.at[k], shard(2 * (m + 1)))
            else:
                rx[k, 0, strip, :] = value

    def reduce_right(k, acc):
        drain(rx.at[k, 1], r_x.at[k, 1])
        for m in range(4):
            place = at(m * 2 + 1 - h, td)
            tb[k, m] = (acc[place, right] + rx[k, 1, place, :]).astype(BF)
        send(tb.at[k], rb.at[k], s_b.at[k], r_b.at[k], shard(1))
        for m in range(4):
            place = at(m * 2 + h, td)
            rx[k, 1, place, :] = acc[place, right] + rx[k, 1, place, :]

    def reduce_cross(k):
        drain(rb.at[k], r_b.at[k])
        for m in range(4):
            over = x ^ ((m + 1) % 4)
            place = at(over * 2 + h, td)
            value = rx[k, 1, place, :] + rb[k, over].astype(F32)
            if m < 3:
                tc[k, m] = value.astype(BF)
                send(tc.at[k, m], rc.at[k, m], s_c.at[k], r_c.at[k], shard(2 * (m + 1)))
            else:
                rx[k, 1, place, :] = value
        drain(ra.at[k], r_a.at[k])
        for e in (1, 0):
            block = rx.at[k, 0, at(t ^ e, td)]
            total = block[...]
            for d in range(3):
                total = total + ra[k, d, at(h ^ e, td), :].astype(F32)
            block[...] = total
            if e == 1:
                send(block, ry.at[k], s_y.at[k], r_y.at[k], shard(1))

    def reduce_done(k, result):
        drain(rc.at[k], r_c.at[k])
        total = rx[k, 1, at(t, td), :]
        for d in range(3):
            total = total + rc[k, d].astype(F32)
        to[k, :, hd:] = total.astype(BF)
        drain(ry.at[k], r_y.at[k])
        to[k, :, :hd] = (rx[k, 0, at(t, td), :] + ry[k]).astype(BF)
        pltpu.make_async_copy(to.at[k], result, l_o.at[k]).start()
        drain(rx.at[k], s_x.at[k])
        drain(ta.at[k], s_a.at[k])
        drain(tb.at[k], s_b.at[k])
        drain(tc.at[k], s_c.at[k])
        drain(ry.at[k], s_y.at[k])

    def fwd_second(i):
        gather_second(h_all.at[i], sd_h.at[i], rv_h.at[i], 3)
        sum_sent(i, 2 * CW)

    def bwd_second(i):
        gather_second(d_all.at[i - nc], sd_dl.at[i - nc], rv_dl.at[i - nc], 2)
        sum_sent(i, CW)

    use = LAG[5]

    def stage(v, lag, fwd, bwd):
        i = v - lag
        pl.when((i >= 0) & (i < nc))(lambda: fwd(i))
        pl.when((i >= nc) & (i < 2 * nc))(lambda: bwd(i))

    @pl.loop(0, 2 * nc + use)
    def _(v):
        stage(
            v, LAG[4],
            lambda i: gather_third(h_all.at[i], sd_h.at[i], rv_h.at[i], 3),
            lambda i: gather_third(d_all.at[i - nc], sd_dl.at[i - nc], rv_dl.at[i - nc], 2),
        )
        stage(
            v, LAG[3],
            fwd_second,
            bwd_second,
        )
        stage(v, LAG[2], fwd_sum, bwd_sum)
        stage(v, LAG[1], lambda i: sum_third(i, 2 * CW), lambda i: sum_third(i, CW))
        stage(v, LAG[0], lambda i: sum_second(i, 2 * CW), lambda i: sum_second(i, CW))
        stage(v, 0, fwd_partial, bwd_partial)

        @pl.when(v == 3)
        def _():
            forward_blocks(1, o_all)
            drain(w_d.at[:, mine], ld_d)
            drain(w_d.at[:, theirs], rv_d)

            @pl.loop(0, nt)
            def _(j):
                x_t[:, at(j, td)] = x_all[at(j, td), :].T

        @pl.when(v == use)
        def _():
            await_blocks(1, o_all)

        stage(v, use, fwd_use, lambda i: bwd_use(i - nc))

        @pl.when(v == nc + use)
        def _():
            reduce_left(0, out_acc)
            reduce_right(0, out_acc)

        @pl.when(v == nc + use + 4)
        def _():
            reduce_cross(0)

        @pl.when(v == nc + use + 7)
        def _():
            reduce_done(0, out)

    reduce_left(1, in_acc)
    reduce_right(1, in_acc)
    reduce_cross(1)
    reduce_done(1, ig)

    for s in range(2):
        drain(st_d.at[s, :, mine], l_dg.at[s])
        drain(st_d.at[s, :, theirs], s_dg.at[s])
        drain(st_gu.at[s, mine], l_gu.at[s])
        drain(st_gu.at[s, theirs], s_gg.at[s])
        drain(to.at[s], l_o.at[s])
    partner = at(oc, fh)
    drain(dg.at[partner, :], r_dg)
    drain(gg.at[:, partner], r_gg.at[0])
    drain(ug.at[:, partner], r_gg.at[1])
    drain(w_gu.at[:, mine], sd_w)
    drain(w_d.at[:, mine], sd_d)
    for k, ref in enumerate((x_all, o_all)):
        drain(ref.at[:, pl.ds(0, dd)], sd_a.at[k])
        drain(ref.at[pl.ds(0, (nt - 1) * td), pl.ds(0, dd)], sf_a.at[k])


PIECES = 4


def hand_over(*refs):
    srcs, dsts, holds, (ins, outs) = refs[:5], refs[5:10], refs[10:15], refs[15:]
    pieces = []
    for j in (2, 3, 4, 0, 1):
        n = srcs[j].shape[0] // PIECES
        for p in range(PIECES):
            place = pl.ds(p * n, n)
            pieces.append((
                pltpu.make_async_copy(srcs[j].at[place], holds[j].at[place], ins.at[j, p]),
                pltpu.make_async_copy(holds[j].at[place], dsts[j].at[place], outs.at[j, p]),
            ))
    for copy, _ in pieces:
        copy.start()
    for copy, leave in pieces:
        copy.wait()
        leave.start()
    for _, leave in pieces:
        leave.wait()


def per_device(tokens, gate_weight, up_weight, down_weight, out_grad):
    nt = lax.axis_size("tensor")
    td, dd = tokens.shape
    ff = gate_weight.shape[1]
    fh = ff // 2
    nc = fh // CW
    n = nt * td
    tq = n // (2 * NZ)
    d2, hd = 2 * dd, dd // 2
    vmem = pltpu.VMEM
    dma = pltpu.SemaphoreType.DMA
    anywhere = pl.BlockSpec(memory_space=pl.ANY)
    results = pl.pallas_call(
        functools.partial(kernel, (nt, td, dd, tq, fh, nc)),
        name="swiglu",
        out_shape=(
            jax.ShapeDtypeStruct((td, dd), BF),
            jax.ShapeDtypeStruct((td, dd), BF),
            jax.ShapeDtypeStruct((dd, ff), BF),
            jax.ShapeDtypeStruct((dd, ff), BF),
            jax.ShapeDtypeStruct((ff, dd), BF),
        ),
        in_specs=[anywhere] * 5,
        out_specs=(anywhere,) * 5,
        scratch_shapes=[
            vmem((nc, d2, 2 * CW), BF),
            vmem((fh, d2), BF),
            vmem((n, d2), BF),
            vmem((d2, n), BF),
            vmem((n, d2), BF),
            vmem((nc, n, CW), BF),
            vmem((nc, n, 2 * CW), BF),
            vmem((n, d2), F32),
            vmem((n, d2), F32),
            vmem((n, 2 * CW), F32),
            vmem((SLOTS, 5, tq, 2 * CW), F32),
            vmem((SLOTS, 3, tq, 2 * CW), BF),
            vmem((SLOTS, 2, tq, 2 * CW), BF),
            vmem((SLOTS, 2, tq, 2 * CW), BF),
            vmem((SLOTS, 3, tq, 2 * CW), BF),
            vmem((SLOTS, 2, tq, 2 * CW), BF),
            vmem((SLOTS, 2, tq, 2 * CW), BF),
            vmem((nc, tq, 2 * CW), F32),
            vmem((2, CW, d2), BF),
            vmem((2, d2, 2 * CW), BF),
            vmem((2, 2, n, hd), F32),
            vmem((2, td, hd), F32),
            vmem((2, 3, 2 * td, hd), BF),
            vmem((2, 3, 2 * td, hd), BF),
            vmem((2, 4, td, hd), BF),
            vmem((2, 4, td, hd), BF),
            vmem((2, 3, td, hd), BF),
            vmem((2, 3, td, hd), BF),
            vmem((2, td, dd), BF),
            dma((nc,)), dma((nc,)), dma,
            dma, dma, dma,
            dma((2,)), dma((2, nt)), dma((2,)), dma((2, nt)), dma((2,)),
            dma((SLOTS,)), dma((SLOTS,)), dma((SLOTS,)),
            dma((SLOTS,)), dma((SLOTS,)), dma((SLOTS,)), dma((SLOTS,)),
            dma((nc,)), dma((nc, 3)), dma((nc,)), dma((nc, 3)),
            dma((2,)), dma((2,)), dma,
            dma((2,)), dma((2,)), dma((2,)),
            dma((2,)), dma((2, 2)), dma((2,)), dma((2,)), dma((2,)), dma((2,)), dma((2,)), dma((2,)), dma((2,)), dma((2,)), dma((2,)),
        ],
        compiler_params=pltpu.CompilerParams(
            collective_id=0, has_side_effects=True, vmem_limit_bytes=63 * 1024 * 1024
        ),
        cost_estimate=pl.CostEstimate(flops=18 * n * d2 * fh, bytes_accessed=6 * ff * dd * 2, transcendentals=0),
    )(tokens, gate_weight, up_weight, down_weight, out_grad)
    return pl.pallas_call(
        hand_over,
        name="hand_over",
        out_shape=tuple(jax.ShapeDtypeStruct(r.shape, r.dtype) for r in results),
        in_specs=[anywhere] * 5,
        out_specs=(anywhere,) * 5,
        scratch_shapes=[vmem(r.shape, r.dtype) for r in results] + [dma((5, PIECES)), dma((5, PIECES))],
        compiler_params=pltpu.CompilerParams(vmem_limit_bytes=60 * 1024 * 1024),
    )(*results)


def solution(mesh):
    act, wide, tall = P("tensor", "pipe"), P("pipe", "tensor"), P("tensor", "pipe")
    return jax.shard_map(
        per_device,
        mesh=mesh,
        in_specs=(act, wide, wide, tall, act),
        out_specs=(act, act, wide, wide, tall),
        check_vma=False,
    )
```

```python
import functools

import jax
import jax.numpy as jnp
from jax import lax
from jax.experimental import pallas as pl
from jax.experimental.pallas import tpu as pltpu
from jax.sharding import PartitionSpec as P

MESH = pl.DeviceIdType.MESH
BF = jnp.bfloat16
F32 = jnp.float32
NZ = 4
CW = 128
SLOTS = 8
LAG = (2, 4, 6, 8, 10, 11)
LATE = (3, 2)


def dot_nn(a, b):
    return lax.dot_general(a, b, (((1,), (0,)), ((), ())), preferred_element_type=F32)


def dot_nt(a, b):
    return lax.dot_general(a, b, (((1,), (1,)), ((), ())), preferred_element_type=F32)


def dot_tn(a, b):
    return lax.dot_general(a, b, (((0,), (0,)), ((), ())), preferred_element_type=F32)


def drain(ref, sem):
    pltpu.make_async_copy(ref, ref, sem).wait()


def kernel(
    dims,
    tok, wg, wu, wd, og,
    out, ig, gg, ug, dg,
    w_gu, w_d, x_all, x_t, o_all, h_all, d_all, out_acc, in_acc, part,
    keep, s1, s2, s3, r1, r2, r3, gu, st_d, st_gu, rx, ry, ta, ra, tb, rb, tc, rc, to,
    ld_w, rv_w, sd_w, ld_d, rv_d, sd_d, ld_a, rv_a, sd_a, rf_a, sf_a,
    free, sd_1, sd_2, sd_3, rv_1, rv_2, rv_3, rv_4, sd_h, rv_h, sd_dl, rv_dl,
    l_dg, s_dg, r_dg, l_gu, s_gg, r_gg, s_x, r_x, s_a, r_a, s_b, r_b, s_c, r_c, s_y, r_y, l_o,
):
    nt, td, dd, tq, fh, nc = dims
    pipe, t = lax.axis_index("pipe"), lax.axis_index("tensor")
    q, c = pipe // 2, pipe % 2
    oc = 1 - c
    tokens = nt * td

    z, y = q // 2, q % 2

    def chip(dz, dy):
        return lax.rem(z + dz + NZ, NZ) * 2 + (y ^ dy)

    up_z, down_z, over_y = ((chip(dz, dy) * 2 + c, t) for dz, dy in ((1, 0), (-1, 0), (0, 1)))

    def shard(d):
        return (pipe, t ^ d)

    other = (q * 2 + oc, t)

    def send(src, dst, s, r, dev):
        pltpu.make_async_remote_copy(
            src_ref=src, dst_ref=dst, send_sem=s, recv_sem=r, device_id=dev, device_id_type=MESH
        ).start()

    def at(i, n):
        return pl.ds(pl.multiple_of(i * n, n), n)

    mine, theirs = at(c, dd), at(oc, dd)

    barrier = pltpu.get_barrier_semaphore()
    for near in (up_z, down_z, over_y):
        pl.semaphore_signal(barrier, inc=1, device_id=near, device_id_type=MESH)
    for d in (1, 2, 4, 6):
        pl.semaphore_signal(barrier, inc=1, device_id=shard(d), device_id_type=MESH)
    pl.semaphore_signal(barrier, inc=1, device_id=other, device_id_type=MESH)
    pl.semaphore_wait(barrier, 8)

    hd = dd // 2
    left = pl.ds(pl.multiple_of(c * dd, hd), hd)
    right = pl.ds(pl.multiple_of(c * dd + hd, hd), hd)

    def spread(k, src, dst):
        place = at(t, td)
        for d, first in ((2, False), (4, False), (6, False), (1, True), (2, True), (4, True), (6, True), (1, False)):
            cols, j = (left, 0) if first else (right, 1)
            send(src.at[:, pl.ds(j * hd, hd)], dst.at[place, cols], sd_a.at[k], rv_a.at[k, d, j], shard(d))
        block = dst.at[place, mine]
        pltpu.make_async_copy(src, block, ld_a.at[k]).start()
        send(src, block, sd_a.at[k], rf_a.at[k, 0, 0], other)

    spread(0, tok, x_all)

    @pl.loop(0, nc)
    def _(i):
        keep_cols = pl.ds(pl.multiple_of(c * fh + i * CW, CW), CW)
        give_cols = pl.ds(pl.multiple_of(oc * fh + i * CW, CW), CW)
        for j, w in enumerate((wg, wu)):
            place = w_gu.at[i, mine, pl.ds(j * CW, CW)]
            pltpu.make_async_copy(w.at[:, keep_cols], place, ld_w.at[i]).start()
            send(w.at[:, give_cols], place, sd_w, rv_w.at[i], other)

    pltpu.make_async_copy(wd.at[at(c, fh), :], w_d.at[:, mine], ld_d).start()
    send(wd.at[at(oc, fh), :], w_d.at[:, mine], sd_d, rv_d, other)

    def forward_blocks(k, ref):
        order = [(1, 0), (2, 1), (4, 1), (6, 1), (2, 0), (4, 0), (6, 0), (1, 1)]
        order += [(3, 0), (3, 1), (5, 0), (5, 1), (7, 0), (7, 1)]
        for d, j in order:
            block = ref.at[at(t ^ d, td), (left, right)[j]]
            drain(block, rv_a.at[k, d, j])
            if (d, j) == (1, 0):
                for e in (2, 4, 6):
                    send(block, block, sd_a.at[k], rv_a.at[k, e + 1, j], shard(e))
            elif d in (2, 4, 6) and j == 1:
                send(block, block, sd_a.at[k], rv_a.at[k, d + 1, j], shard(1))
            send(block, block, sf_a.at[k], rf_a.at[k, d, j], other)

    def await_blocks(k, ref):
        drain(ref.at[at(t, td), mine], ld_a.at[k])
        drain(ref.at[at(t, td), theirs], rf_a.at[k, 0, 0])
        for d in range(1, nt):
            for j in range(2):
                cols = pl.ds(pl.multiple_of(oc * dd + j * hd, hd), hd)
                drain(ref.at[at(t ^ d, td), cols], rf_a.at[k, d, j])

    forward_blocks(0, x_all)
    spread(1, og, o_all)
    await_blocks(0, x_all)

    half = tokens // 2

    hq = tq // 2
    low, high = pl.ds(0, hq), pl.ds(hq, hq)

    def sum_first(v, width):
        slot, w = lax.rem(v, SLOTS), pl.ds(0, width)

        @pl.when(v >= SLOTS)
        def _():
            for j in range(3):
                pl.semaphore_wait(free.at[j], 1)

        for j, (dz, dy) in enumerate(((0, 0), (1, 0), (-1, 0), (2, 0), (0, 1))):
            keep[slot, j, :, w] = part[at(chip(dz, dy), tq), w]
        for j, (dz, dev) in enumerate(((2, over_y), (1, up_z), (-1, down_z))):
            s1[slot, j, :, w] = part[at(chip(dz, 1), tq), w].astype(BF)
            send(s1.at[slot, j, :, w], r1.at[slot, j, :, w], sd_1.at[slot], rv_1.at[slot], dev)

    def sum_second(v, width):
        slot, w = lax.rem(v, SLOTS), pl.ds(0, width)
        drain(r1.at[slot, :, :, w], rv_1.at[slot])
        s2[slot, 0, :, w] = (keep[slot, 3, :, w] + r1[slot, 0, :, w].astype(F32)).astype(BF)
        s2[slot, 1, :, w] = (
            keep[slot, 4, :, w] + r1[slot, 1, :, w].astype(F32) + r1[slot, 2, :, w].astype(F32)
        ).astype(BF)
        for rows, dev in ((low, down_z), (high, up_z)):
            send(s2.at[slot, 0, rows, w], r2.at[slot, 0, rows, w], sd_2.at[slot], rv_2.at[slot], dev)
        send(s2.at[slot, 1, :, w], r2.at[slot, 1, :, w], sd_2.at[slot], rv_3.at[slot], over_y)

    def sum_third(v, width):
        slot, w = lax.rem(v, SLOTS), pl.ds(0, width)
        drain(r2.at[slot, 0, :, w], rv_2.at[slot])
        s3[slot, 0, low, w] = (keep[slot, 2, low, w] + r2[slot, 0, low, w].astype(F32)).astype(BF)
        s3[slot, 0, high, w] = keep[slot, 2, high, w].astype(BF)
        s3[slot, 1, low, w] = keep[slot, 1, low, w].astype(BF)
        s3[slot, 1, high, w] = (keep[slot, 1, high, w] + r2[slot, 0, high, w].astype(F32)).astype(BF)
        for j, dev in enumerate((down_z, up_z)):
            send(s3.at[slot, j, :, w], r3.at[slot, j, :, w], sd_3.at[slot], rv_4.at[slot], dev)

    def sum_total(v, width):
        slot, w = lax.rem(v, SLOTS), pl.ds(0, width)
        drain(r2.at[slot, 1, :, w], rv_3.at[slot])
        drain(r3.at[slot, :, :, w], rv_4.at[slot])
        total = (keep[slot, 0, :, w] + r2[slot, 1, :, w].astype(F32)) + (
            r3[slot, 0, :, w].astype(F32) + r3[slot, 1, :, w].astype(F32)
        )

        @pl.when(v < 2 * nc - SLOTS)
        def _():
            for j, dev in enumerate((down_z, up_z, over_y)):
                pl.semaphore_signal(free.at[j], inc=1, device_id=dev, device_id_type=MESH)

        return total

    def sum_sent(v, width):
        slot, w = lax.rem(v, SLOTS), pl.ds(0, width)
        drain(s1.at[slot, :, :, w], sd_1.at[slot])
        drain(s2.at[slot, :, :, w], sd_2.at[slot])
        drain(s3.at[slot, :, :, w], sd_3.at[slot])

    def gather_first(ref, sd, rv):
        block = ref.at[at(q, tq)]
        for dev in (up_z, down_z, over_y):
            send(block, block, sd, rv.at[0], dev)

    def gather_second(ref, sd, rv, crossings):
        drain(ref.at[pl.ds(0, 3 * tq)], rv.at[0])
        below, above, beside = (chip(dz, dy) * tq for dz, dy in ((-1, 0), (1, 0), (0, 1)))
        moves = [(below, hq, up_z), (above + hq, hq, down_z)]
        if crossings == 3:
            moves += [(below, tq, over_y), (above, tq, over_y)]
        else:
            moves += [(beside, tq, up_z), (beside, tq, down_z)]
        for first, n, dev in moves:
            block = ref.at[pl.ds(pl.multiple_of(first, hq), n)]
            send(block, block, sd, rv.at[1], dev)

    def gather_third(ref, sd, rv, crossings):
        drain(ref.at[pl.ds(0, 3 * tq)], rv.at[1])
        if crossings == 3:
            moves = [(chip(-1, 1) * tq, hq, up_z), (chip(1, 1) * tq + hq, hq, down_z)]
        else:
            moves = [(chip(2, 0) * tq, tq, over_y)]
        for first, n, dev in moves:
            block = ref.at[pl.ds(pl.multiple_of(first, hq), n)]
            send(block, block, sd, rv.at[2], dev)

    def gather_done(ref, sd, rv):
        drain(ref.at[pl.ds(0, tq)], rv.at[2])
        drain(ref.at[pl.ds(0, 7 * tq)], sd)

    def col_block(m):
        return pl.ds(pl.multiple_of(((oc * 2 + 1 - m % 2 + m // 2 * 2) % 4) * hd, hd), hd)

    def h_of(i):
        return h_all.at[i // 2, :, at(i % 2, CW)]

    def fwd_partial(v):
        drain(w_gu.at[v, mine], ld_w.at[v])
        drain(w_gu.at[v, theirs], rv_w.at[v])

        @pl.loop(0, 2)
        def _(m):
            part[at(m, half), :] = dot_nn(x_all[at(m, half), :], w_gu[v])

        sum_first(v, 2 * CW)

    def fwd_sum(v):
        total = sum_total(v, 2 * CW)
        gu[v] = total
        gate, up = total[:, :CW], total[:, CW:]
        block = h_of(v).at[at(q, tq)]
        block[...] = (gate * jax.nn.sigmoid(gate) * up).astype(BF)
        gather_first(h_of(v), sd_h.at[v], rv_h.at[v])

    def fwd_use(i):
        gather_done(h_of(i), sd_h.at[i], rv_h.at[i])
        pl.when(i % 2 == 1)(lambda: fwd_pair(i // 2))

    def fwd_pair(p):
        @pl.loop(0, 4)
        def _(m):
            cols = col_block(m)
            value = dot_nn(h_all[p], w_d[at(p, 2 * CW), cols])

            @pl.when(p == 0)
            def _():
                out_acc[:, cols] = value

            @pl.when(p > 0)
            def _():
                out_acc[:, cols] += value

            @pl.when((p == nc // 2 - 1) & (m < 2))
            def _():
                send(out_acc.at[:, cols], rx.at[0, m], s_x.at[0], r_x.at[0, m], other)

        s = lax.rem(p, 2)
        place = pl.ds(pl.multiple_of(c * fh + p * (2 * CW), CW), 2 * CW)

        @pl.when(p >= 2)
        def _():
            drain(st_d.at[s, :, mine], l_dg.at[s])
            drain(st_d.at[s, :, theirs], s_dg.at[s])

        st_d[s] = dot_tn(h_all[p], o_all[...]).astype(BF)
        pltpu.make_async_copy(st_d.at[s, :, mine], dg.at[place, :], l_dg.at[s]).start()
        send(st_d.at[s, :, theirs], dg.at[place, :], s_dg.at[s], r_dg, other)

    def bwd_partial(v):
        @pl.loop(0, 2)
        def _(m):
            part[at(m, half), pl.ds(0, CW)] = dot_nt(o_all[at(m, half), :], w_d[at(v - nc, CW), :])

        sum_first(v, CW)

    def bwd_sum(v):
        total = sum_total(v, CW)
        i = v - nc
        gate, up = gu[i, :, :CW], gu[i, :, CW:]
        sigma = jax.nn.sigmoid(gate)
        d_all[i, at(q, tq), :CW] = (total * up * sigma * (1.0 + gate * (1.0 - sigma))).astype(BF)
        d_all[i, at(q, tq), CW:] = (total * (gate * sigma)).astype(BF)
        gather_first(d_all.at[i], sd_dl.at[i], rv_dl.at[i])

    def bwd_use(i):
        gather_done(d_all.at[i], sd_dl.at[i], rv_dl.at[i])

        @pl.loop(0, 4)
        def _(m):
            cols = col_block(m)
            value = dot_nt(d_all[i], w_gu[i, cols, :])

            @pl.when(i == 0)
            def _():
                in_acc[:, cols] = value

            @pl.when(i > 0)
            def _():
                in_acc[:, cols] += value

            @pl.when((i == nc - 1) & (m < 2))
            def _():
                send(in_acc.at[:, cols], rx.at[1, m], s_x.at[1], r_x.at[1, m], other)

        pl.when(i < nc - sum(LATE))(lambda: weight_grads(i))

    def weight_grads(i):
        s = lax.rem(i, 2)
        place = pl.ds(pl.multiple_of(c * fh + i * CW, CW), CW)

        @pl.when(i >= 2)
        def _():
            drain(st_gu.at[s, mine], l_gu.at[s])
            drain(st_gu.at[s, theirs], s_gg.at[s])

        @pl.loop(0, 2)
        def _(m):
            st_gu[s, at(m, dd), :] = dot_nn(x_t[at(m, dd), :], d_all[i]).astype(BF)

        for j, (grad, r) in enumerate(((gg, 0), (ug, 1))):
            lanes = pl.ds(j * CW, CW)
            pltpu.make_async_copy(st_gu.at[s, mine, lanes], grad.at[:, place], l_gu.at[s]).start()
            send(st_gu.at[s, theirs, lanes], grad.at[:, place], s_gg.at[s], r_gg.at[r], other)

    x, h = t // 2, t % 2

    def reduce_left(k, acc):
        drain(rx.at[k, 1], r_x.at[k, 1])
        for m in range(4):
            strip = at(x ^ ((m + 1) % 4), 2 * td)
            value = acc[strip, left] + rx[k, 1, strip, :]
            if m < 3:
                ta[k, m] = value.astype(BF)
                send(ta.at[k, m], ra.at[k, m], s_a.at[k], r_a.at[k], shard(2 * (m + 1)))
            else:
                rx[k, 1, strip, :] = value

    def reduce_right(k, acc):
        drain(rx.at[k, 0], r_x.at[k, 0])
        for m in range(4):
            place = at(m * 2 + 1 - h, td)
            tb[k, m] = (acc[place, right] + rx[k, 0, place, :]).astype(BF)
        send(tb.at[k], rb.at[k], s_b.at[k], r_b.at[k], shard(1))
        for m in range(4):
            place = at(m * 2 + h, td)
            rx[k, 0, place, :] = acc[place, right] + rx[k, 0, place, :]

    def reduce_cross(k):
        drain(rb.at[k], r_b.at[k])
        for m in range(4):
            over = x ^ ((m + 1) % 4)
            place = at(over * 2 + h, td)
            value = rx[k, 0, place, :] + rb[k, over].astype(F32)
            if m < 3:
                tc[k, m] = value.astype(BF)
                send(tc.at[k, m], rc.at[k, m], s_c.at[k], r_c.at[k], shard(2 * (m + 1)))
            else:
                rx[k, 0, place, :] = value
        drain(ra.at[k], r_a.at[k])
        for e in (1, 0):
            block = rx.at[k, 1, at(t ^ e, td)]
            total = block[...]
            for d in range(3):
                total = total + ra[k, d, at(h ^ e, td), :].astype(F32)
            block[...] = total
            if e == 1:
                send(block, ry.at[k], s_y.at[k], r_y.at[k], shard(1))

    def reduce_done(k, result):
        drain(rc.at[k], r_c.at[k])
        total = rx[k, 0, at(t, td), :]
        for d in range(3):
            total = total + rc[k, d].astype(F32)
        to[k, :, hd:] = total.astype(BF)
        drain(ry.at[k], r_y.at[k])
        to[k, :, :hd] = (rx[k, 1, at(t, td), :] + ry[k]).astype(BF)
        pltpu.make_async_copy(to.at[k], result, l_o.at[k]).start()
        drain(rx.at[k], s_x.at[k])
        drain(ta.at[k], s_a.at[k])
        drain(tb.at[k], s_b.at[k])
        drain(tc.at[k], s_c.at[k])
        drain(ry.at[k], s_y.at[k])

    use = LAG[5]

    def stage(v, lag, fwd, bwd):
        i = v - lag
        pl.when((i >= 0) & (i < nc))(lambda: fwd(i))
        pl.when((i >= nc) & (i < 2 * nc))(lambda: bwd(i))

    @pl.loop(0, 2 * nc + use)
    def _(v):
        stage(v, 0, fwd_partial, bwd_partial)
        stage(
            v, LAG[4],
            lambda i: gather_third(h_of(i), sd_h.at[i], rv_h.at[i], 3),
            lambda i: gather_third(d_all.at[i - nc], sd_dl.at[i - nc], rv_dl.at[i - nc], 2),
        )
        stage(
            v, LAG[3],
            lambda i: gather_second(h_of(i), sd_h.at[i], rv_h.at[i], 3),
            lambda i: gather_second(d_all.at[i - nc], sd_dl.at[i - nc], rv_dl.at[i - nc], 2),
        )
        stage(v, LAG[2], fwd_sum, bwd_sum)
        stage(v, LAG[2] + 1, lambda i: sum_sent(i, 2 * CW), lambda i: sum_sent(i, CW))
        stage(v, LAG[1], lambda i: sum_third(i, 2 * CW), lambda i: sum_third(i, CW))
        stage(v, LAG[0], lambda i: sum_second(i, 2 * CW), lambda i: sum_second(i, CW))

        @pl.when(v == use - 4)
        def _():
            forward_blocks(1, o_all)

        @pl.when(v == use)
        def _():
            await_blocks(1, o_all)
            drain(w_d.at[:, mine], ld_d)
            drain(w_d.at[:, theirs], rv_d)

        @pl.when((v >= nc) & (v < nc + nt))
        def _():
            x_t[:, at(v - nc, td)] = x_all[at(v - nc, td), :].T

        stage(v, use, fwd_use, lambda i: bwd_use(i - nc))

        @pl.when(v == nc + use)
        def _():
            reduce_right(0, out_acc)
            reduce_left(0, out_acc)

        @pl.when(v == nc + use + 4)
        def _():
            reduce_cross(0)

        @pl.when(v == nc + use + 7)
        def _():
            reduce_done(0, out)

    reduce_right(1, in_acc)
    reduce_left(1, in_acc)
    pl.loop(nc - sum(LATE), nc - LATE[1])(weight_grads)
    reduce_cross(1)
    pl.loop(nc - LATE[1], nc)(weight_grads)
    reduce_done(1, ig)

    for s in range(2):
        drain(st_d.at[s, :, mine], l_dg.at[s])
        drain(st_d.at[s, :, theirs], s_dg.at[s])
        drain(st_gu.at[s, mine], l_gu.at[s])
        drain(st_gu.at[s, theirs], s_gg.at[s])
        drain(to.at[s], l_o.at[s])
    partner = at(oc, fh)
    drain(dg.at[partner, :], r_dg)
    drain(gg.at[:, partner], r_gg.at[0])
    drain(ug.at[:, partner], r_gg.at[1])
    drain(w_gu.at[:, mine], sd_w)
    drain(w_d.at[:, mine], sd_d)
    for k, ref in enumerate((x_all, o_all)):
        drain(ref.at[:, pl.ds(0, dd)], sd_a.at[k])
        drain(ref.at[pl.ds(0, (nt - 1) * td), pl.ds(0, dd)], sf_a.at[k])


PIECES = 4


def hand_over(*refs):
    srcs, dsts, holds, (ins, outs) = refs[:5], refs[5:10], refs[10:15], refs[15:]
    pieces = []
    for j in (2, 3, 4, 0, 1):
        n = srcs[j].shape[0] // PIECES
        for p in range(PIECES):
            place = pl.ds(p * n, n)
            pieces.append((
                pltpu.make_async_copy(srcs[j].at[place], holds[j].at[place], ins.at[j, p]),
                pltpu.make_async_copy(holds[j].at[place], dsts[j].at[place], outs.at[j, p]),
            ))
    for copy, _ in pieces:
        copy.start()
    for copy, leave in pieces:
        copy.wait()
        leave.start()
    for _, leave in pieces:
        leave.wait()


def per_device(tokens, gate_weight, up_weight, down_weight, out_grad):
    nt = lax.axis_size("tensor")
    td, dd = tokens.shape
    ff = gate_weight.shape[1]
    fh = ff // 2
    nc = fh // CW
    n = nt * td
    tq = n // (2 * NZ)
    d2, hd = 2 * dd, dd // 2
    vmem = pltpu.VMEM
    dma = pltpu.SemaphoreType.DMA
    anywhere = pl.BlockSpec(memory_space=pl.ANY)
    results = pl.pallas_call(
        functools.partial(kernel, (nt, td, dd, tq, fh, nc)),
        name="swiglu",
        out_shape=(
            jax.ShapeDtypeStruct((td, dd), BF),
            jax.ShapeDtypeStruct((td, dd), BF),
            jax.ShapeDtypeStruct((dd, ff), BF),
            jax.ShapeDtypeStruct((dd, ff), BF),
            jax.ShapeDtypeStruct((ff, dd), BF),
        ),
        in_specs=[anywhere] * 5,
        out_specs=(anywhere,) * 5,
        scratch_shapes=[
            vmem((nc, d2, 2 * CW), BF),
            vmem((fh, d2), BF),
            vmem((n, d2), BF),
            vmem((d2, n), BF),
            vmem((n, d2), BF),
            vmem((nc // 2, n, 2 * CW), BF),
            vmem((nc, n, 2 * CW), BF),
            vmem((n, d2), F32),
            vmem((n, d2), F32),
            vmem((n, 2 * CW), F32),
            vmem((SLOTS, 5, tq, 2 * CW), F32),
            vmem((SLOTS, 3, tq, 2 * CW), BF),
            vmem((SLOTS, 2, tq, 2 * CW), BF),
            vmem((SLOTS, 2, tq, 2 * CW), BF),
            vmem((SLOTS, 3, tq, 2 * CW), BF),
            vmem((SLOTS, 2, tq, 2 * CW), BF),
            vmem((SLOTS, 2, tq, 2 * CW), BF),
            vmem((nc, tq, 2 * CW), F32),
            vmem((2, 2 * CW, d2), BF),
            vmem((2, d2, 2 * CW), BF),
            vmem((2, 2, n, hd), F32),
            vmem((2, td, hd), F32),
            vmem((2, 3, 2 * td, hd), BF),
            vmem((2, 3, 2 * td, hd), BF),
            vmem((2, 4, td, hd), BF),
            vmem((2, 4, td, hd), BF),
            vmem((2, 3, td, hd), BF),
            vmem((2, 3, td, hd), BF),
            vmem((2, td, dd), BF),
            dma((nc,)), dma((nc,)), dma,
            dma, dma, dma,
            dma((2,)), dma((2, nt, 2)), dma((2,)), dma((2, nt, 2)), dma((2,)),
            pltpu.SemaphoreType.REGULAR((3,)),
            dma((SLOTS,)), dma((SLOTS,)), dma((SLOTS,)),
            dma((SLOTS,)), dma((SLOTS,)), dma((SLOTS,)), dma((SLOTS,)),
            dma((nc,)), dma((nc, 3)), dma((nc,)), dma((nc, 3)),
            dma((2,)), dma((2,)), dma,
            dma((2,)), dma((2,)), dma((2,)),
            dma((2,)), dma((2, 2)), dma((2,)), dma((2,)), dma((2,)), dma((2,)), dma((2,)), dma((2,)), dma((2,)), dma((2,)), dma((2,)),
        ],
        compiler_params=pltpu.CompilerParams(
            collective_id=0, has_side_effects=True, vmem_limit_bytes=63 * 1024 * 1024
        ),
        cost_estimate=pl.CostEstimate(flops=18 * n * d2 * fh, bytes_accessed=6 * ff * dd * 2, transcendentals=0),
    )(tokens, gate_weight, up_weight, down_weight, out_grad)
    return pl.pallas_call(
        hand_over,
        name="hand_over",
        out_shape=tuple(jax.ShapeDtypeStruct(r.shape, r.dtype) for r in results),
        in_specs=[anywhere] * 5,
        out_specs=(anywhere,) * 5,
        scratch_shapes=[vmem(r.shape, r.dtype) for r in results] + [dma((5, PIECES)), dma((5, PIECES))],
        compiler_params=pltpu.CompilerParams(vmem_limit_bytes=60 * 1024 * 1024),
    )(*results)


def solution(mesh):
    act, wide, tall = P("tensor", "pipe"), P("pipe", "tensor"), P("tensor", "pipe")
    return jax.shard_map(
        per_device,
        mesh=mesh,
        in_specs=(act, wide, wide, tall, act),
        out_specs=(act, act, wide, wide, tall),
        check_vma=False,
    )
```

```python
import functools

import jax
import jax.numpy as jnp
from jax import lax
from jax.experimental import pallas as pl
from jax.experimental.pallas import tpu as pltpu
from jax.sharding import PartitionSpec as P

MESH = pl.DeviceIdType.MESH
BF = jnp.bfloat16
F32 = jnp.float32
NZ = 4
CW = 128
SLOTS = 8
LAG = (2, 4, 6, 8, 10, 11)
LATE = (3, 2)


def dot_nn(a, b):
    return lax.dot_general(a, b, (((1,), (0,)), ((), ())), preferred_element_type=F32)


def dot_nt(a, b):
    return lax.dot_general(a, b, (((1,), (1,)), ((), ())), preferred_element_type=F32)


def dot_tn(a, b):
    return lax.dot_general(a, b, (((0,), (0,)), ((), ())), preferred_element_type=F32)


def drain(ref, sem):
    pltpu.make_async_copy(ref, ref, sem).wait()


def kernel(
    dims,
    tok, wg, wu, wd, og,
    out, ig, gg, ug, dg,
    w_gu, w_d, x_all, x_t, o_all, h_all, d_all, out_acc, in_acc, part,
    keep, s1, s2, s3, r1, r2, r3, gu, st_d, st_gu, rx, ry, ta, ra, tb, rb, tc, rc, to,
    ld_w, rv_w, sd_w, ld_d, rv_d, sd_d, ld_a, rv_a, sd_a, rf_a, sf_a,
    free, sd_1, sd_2, sd_3, rv_1, rv_2, rv_3, rv_4, sd_h, rv_h, sd_dl, rv_dl,
    l_dg, s_dg, r_dg, l_gu, s_gg, r_gg, s_x, r_x, s_a, r_a, s_b, r_b, s_c, r_c, s_y, r_y, l_o,
):
    nt, td, dd, tq, fh, nc = dims
    pipe, t = lax.axis_index("pipe"), lax.axis_index("tensor")
    q, c = pipe // 2, pipe % 2
    oc = 1 - c
    tokens = nt * td

    z, y = q // 2, q % 2

    def chip(dz, dy):
        return lax.rem(z + dz + NZ, NZ) * 2 + (y ^ dy)

    up_z, down_z, over_y = ((chip(dz, dy) * 2 + c, t) for dz, dy in ((1, 0), (-1, 0), (0, 1)))

    def shard(d):
        return (pipe, t ^ d)

    other = (q * 2 + oc, t)

    def send(src, dst, s, r, dev):
        pltpu.make_async_remote_copy(
            src_ref=src, dst_ref=dst, send_sem=s, recv_sem=r, device_id=dev, device_id_type=MESH
        ).start()

    def at(i, n):
        return pl.ds(pl.multiple_of(i * n, n), n)

    mine, theirs = at(c, dd), at(oc, dd)

    barrier = pltpu.get_barrier_semaphore()
    for near in (up_z, down_z, over_y):
        pl.semaphore_signal(barrier, inc=1, device_id=near, device_id_type=MESH)
    for d in (1, 2, 4, 6):
        pl.semaphore_signal(barrier, inc=1, device_id=shard(d), device_id_type=MESH)
    pl.semaphore_signal(barrier, inc=1, device_id=other, device_id_type=MESH)
    pl.semaphore_wait(barrier, 8)

    hd = dd // 2
    left = pl.ds(pl.multiple_of(c * dd, hd), hd)
    right = pl.ds(pl.multiple_of(c * dd + hd, hd), hd)

    def spread(k, src, dst):
        place = at(t, td)
        for d, first in ((2, False), (4, False), (6, False), (1, True), (2, True), (4, True), (6, True), (1, False)):
            cols, j = (left, 0) if first else (right, 1)
            send(src.at[:, pl.ds(j * hd, hd)], dst.at[place, cols], sd_a.at[k], rv_a.at[k, d, j], shard(d))
        block = dst.at[place, mine]
        pltpu.make_async_copy(src, block, ld_a.at[k]).start()
        send(src, block, sd_a.at[k], rf_a.at[k, 0, 0], other)

    spread(0, tok, x_all)

    @pl.loop(0, nc)
    def _(i):
        keep_cols = pl.ds(pl.multiple_of(c * fh + i * CW, CW), CW)
        give_cols = pl.ds(pl.multiple_of(oc * fh + i * CW, CW), CW)
        for j, w in enumerate((wg, wu)):
            place = w_gu.at[i, mine, pl.ds(j * CW, CW)]
            pltpu.make_async_copy(w.at[:, keep_cols], place, ld_w.at[i]).start()
            send(w.at[:, give_cols], place, sd_w, rv_w.at[i], other)

    pltpu.make_async_copy(wd.at[at(c, fh), :], w_d.at[:, mine], ld_d).start()
    send(wd.at[at(oc, fh), :], w_d.at[:, mine], sd_d, rv_d, other)

    def forward_blocks(k, ref):
        order = [(1, 0), (2, 1), (4, 1), (6, 1), (2, 0), (4, 0), (6, 0), (1, 1)]
        order += [(3, 0), (3, 1), (5, 0), (5, 1), (7, 0), (7, 1)]
        for d, j in order:
            block = ref.at[at(t ^ d, td), (left, right)[j]]
            drain(block, rv_a.at[k, d, j])
            if d == 1 and (j == 0 or k == 1):
                for e in (2, 4, 6):
                    send(block, block, sd_a.at[k], rv_a.at[k, e + 1, j], shard(e))
            elif d in (2, 4, 6) and j == 1 and k == 0:
                send(block, block, sd_a.at[k], rv_a.at[k, d + 1, j], shard(1))
            send(block, block, sf_a.at[k], rf_a.at[k, d, j], other)

    def await_blocks(k, ref):
        drain(ref.at[at(t, td), mine], ld_a.at[k])
        drain(ref.at[at(t, td), theirs], rf_a.at[k, 0, 0])
        for d in range(1, nt):
            for j in range(2):
                cols = pl.ds(pl.multiple_of(oc * dd + j * hd, hd), hd)
                drain(ref.at[at(t ^ d, td), cols], rf_a.at[k, d, j])

    forward_blocks(0, x_all)
    spread(1, og, o_all)
    await_blocks(0, x_all)

    half = tokens // 2

    hq = tq // 2
    low, high = pl.ds(0, hq), pl.ds(hq, hq)

    def sum_first(v, width):
        slot, w = lax.rem(v, SLOTS), pl.ds(0, width)

        @pl.when(v >= SLOTS)
        def _():
            for j in range(3):
                pl.semaphore_wait(free.at[j], 1)

        for j, (dz, dy) in enumerate(((0, 0), (1, 0), (-1, 0), (2, 0), (0, 1))):
            keep[slot, j, :, w] = part[at(chip(dz, dy), tq), w]
        for j, (dz, dev) in enumerate(((2, over_y), (1, up_z), (-1, down_z))):
            s1[slot, j, :, w] = part[at(chip(dz, 1), tq), w].astype(BF)
            send(s1.at[slot, j, :, w], r1.at[slot, j, :, w], sd_1.at[slot], rv_1.at[slot], dev)

    def sum_second(v, width):
        slot, w = lax.rem(v, SLOTS), pl.ds(0, width)
        drain(r1.at[slot, :, :, w], rv_1.at[slot])
        s2[slot, 0, :, w] = (keep[slot, 3, :, w] + r1[slot, 0, :, w].astype(F32)).astype(BF)
        s2[slot, 1, :, w] = (
            keep[slot, 4, :, w] + r1[slot, 1, :, w].astype(F32) + r1[slot, 2, :, w].astype(F32)
        ).astype(BF)
        for rows, dev in ((low, down_z), (high, up_z)):
            send(s2.at[slot, 0, rows, w], r2.at[slot, 0, rows, w], sd_2.at[slot], rv_2.at[slot], dev)
        send(s2.at[slot, 1, :, w], r2.at[slot, 1, :, w], sd_2.at[slot], rv_3.at[slot], over_y)

    def sum_third(v, width):
        slot, w = lax.rem(v, SLOTS), pl.ds(0, width)
        drain(r2.at[slot, 0, :, w], rv_2.at[slot])
        s3[slot, 0, low, w] = (keep[slot, 2, low, w] + r2[slot, 0, low, w].astype(F32)).astype(BF)
        s3[slot, 0, high, w] = keep[slot, 2, high, w].astype(BF)
        s3[slot, 1, low, w] = keep[slot, 1, low, w].astype(BF)
        s3[slot, 1, high, w] = (keep[slot, 1, high, w] + r2[slot, 0, high, w].astype(F32)).astype(BF)
        for j, dev in enumerate((down_z, up_z)):
            send(s3.at[slot, j, :, w], r3.at[slot, j, :, w], sd_3.at[slot], rv_4.at[slot], dev)

    def sum_total(v, width):
        slot, w = lax.rem(v, SLOTS), pl.ds(0, width)
        drain(r2.at[slot, 1, :, w], rv_3.at[slot])
        drain(r3.at[slot, :, :, w], rv_4.at[slot])
        total = (keep[slot, 0, :, w] + r2[slot, 1, :, w].astype(F32)) + (
            r3[slot, 0, :, w].astype(F32) + r3[slot, 1, :, w].astype(F32)
        )

        @pl.when(v < 2 * nc - SLOTS)
        def _():
            for j, dev in enumerate((down_z, up_z, over_y)):
                pl.semaphore_signal(free.at[j], inc=1, device_id=dev, device_id_type=MESH)

        return total

    def sum_sent(v, width):
        slot, w = lax.rem(v, SLOTS), pl.ds(0, width)
        drain(s1.at[slot, :, :, w], sd_1.at[slot])
        drain(s2.at[slot, :, :, w], sd_2.at[slot])
        drain(s3.at[slot, :, :, w], sd_3.at[slot])

    def gather_first(ref, sd, rv):
        block = ref.at[at(q, tq)]
        for dev in (up_z, down_z, over_y):
            send(block, block, sd, rv.at[0], dev)

    def gather_second(ref, sd, rv, crossings):
        drain(ref.at[pl.ds(0, 3 * tq)], rv.at[0])
        below, above, beside = (chip(dz, dy) * tq for dz, dy in ((-1, 0), (1, 0), (0, 1)))
        moves = [(below, hq, up_z), (above + hq, hq, down_z)]
        if crossings == 3:
            moves += [(below, tq, over_y), (above, tq, over_y)]
        else:
            moves += [(beside, tq, up_z), (beside, tq, down_z)]
        for first, n, dev in moves:
            block = ref.at[pl.ds(pl.multiple_of(first, hq), n)]
            send(block, block, sd, rv.at[1], dev)

    def gather_third(ref, sd, rv, crossings):
        drain(ref.at[pl.ds(0, 3 * tq)], rv.at[1])
        if crossings == 3:
            moves = [(chip(-1, 1) * tq, hq, up_z), (chip(1, 1) * tq + hq, hq, down_z)]
        else:
            moves = [(chip(2, 0) * tq, tq, over_y)]
        for first, n, dev in moves:
            block = ref.at[pl.ds(pl.multiple_of(first, hq), n)]
            send(block, block, sd, rv.at[2], dev)

    def gather_done(ref, sd, rv):
        drain(ref.at[pl.ds(0, tq)], rv.at[2])
        drain(ref.at[pl.ds(0, 7 * tq)], sd)

    def col_block(m):
        return pl.ds(pl.multiple_of(((oc * 2 + 1 - m % 2 + m // 2 * 2) % 4) * hd, hd), hd)

    def h_of(i):
        return h_all.at[i // 2, :, at(i % 2, CW)]

    def fwd_partial(v):
        drain(w_gu.at[v, mine], ld_w.at[v])
        drain(w_gu.at[v, theirs], rv_w.at[v])

        @pl.loop(0, 2)
        def _(m):
            part[at(m, half), :] = dot_nn(x_all[at(m, half), :], w_gu[v])

        sum_first(v, 2 * CW)

    def fwd_sum(v):
        total = sum_total(v, 2 * CW)
        gu[v] = total
        gate, up = total[:, :CW], total[:, CW:]
        block = h_of(v).at[at(q, tq)]
        block[...] = (gate * jax.nn.sigmoid(gate) * up).astype(BF)
        gather_first(h_of(v), sd_h.at[v], rv_h.at[v])

    def fwd_use(i):
        gather_done(h_of(i), sd_h.at[i], rv_h.at[i])
        pl.when(i % 2 == 1)(lambda: fwd_pair(i // 2))

    def fwd_pair(p):
        @pl.loop(0, 4)
        def _(m):
            cols = col_block(m)
            value = dot_nn(h_all[p], w_d[at(p, 2 * CW), cols])

            @pl.when(p == 0)
            def _():
                out_acc[:, cols] = value

            @pl.when(p > 0)
            def _():
                out_acc[:, cols] += value

            @pl.when((p == nc // 2 - 1) & (m < 2))
            def _():
                send(out_acc.at[:, cols], rx.at[0, m], s_x.at[0], r_x.at[0, m], other)

        s = lax.rem(p, 2)
        place = pl.ds(pl.multiple_of(c * fh + p * (2 * CW), CW), 2 * CW)

        @pl.when(p >= 2)
        def _():
            drain(st_d.at[s, :, mine], l_dg.at[s])
            drain(st_d.at[s, :, theirs], s_dg.at[s])

        st_d[s] = dot_tn(h_all[p], o_all[...]).astype(BF)
        pltpu.make_async_copy(st_d.at[s, :, mine], dg.at[place, :], l_dg.at[s]).start()
        send(st_d.at[s, :, theirs], dg.at[place, :], s_dg.at[s], r_dg, other)

    def bwd_partial(v):
        @pl.loop(0, 2)
        def _(m):
            part[at(m, half), pl.ds(0, CW)] = dot_nt(o_all[at(m, half), :], w_d[at(v - nc, CW), :])

        sum_first(v, CW)

    def bwd_sum(v):
        total = sum_total(v, CW)
        i = v - nc
        gate, up = gu[i, :, :CW], gu[i, :, CW:]
        sigma = jax.nn.sigmoid(gate)
        d_all[i, at(q, tq), :CW] = (total * up * sigma * (1.0 + gate * (1.0 - sigma))).astype(BF)
        d_all[i, at(q, tq), CW:] = (total * (gate * sigma)).astype(BF)
        gather_first(d_all.at[i], sd_dl.at[i], rv_dl.at[i])

    def bwd_use(i):
        gather_done(d_all.at[i], sd_dl.at[i], rv_dl.at[i])

        @pl.loop(0, 4)
        def _(m):
            cols = col_block(m)
            value = dot_nt(d_all[i], w_gu[i, cols, :])

            @pl.when(i == 0)
            def _():
                in_acc[:, cols] = value

            @pl.when(i > 0)
            def _():
                in_acc[:, cols] += value

            @pl.when((i == nc - 1) & (m < 2))
            def _():
                send(in_acc.at[:, cols], rx.at[1, m], s_x.at[1], r_x.at[1, m], other)

        pl.when(i < nc - sum(LATE))(lambda: weight_grads(i))

    def weight_grads(i):
        s = lax.rem(i, 2)
        place = pl.ds(pl.multiple_of(c * fh + i * CW, CW), CW)

        @pl.when(i >= 2)
        def _():
            drain(st_gu.at[s, mine], l_gu.at[s])
            drain(st_gu.at[s, theirs], s_gg.at[s])

        @pl.loop(0, 2)
        def _(m):
            st_gu[s, at(m, dd), :] = dot_nn(x_t[at(m, dd), :], d_all[i]).astype(BF)

        for j, (grad, r) in enumerate(((gg, 0), (ug, 1))):
            lanes = pl.ds(j * CW, CW)
            pltpu.make_async_copy(st_gu.at[s, mine, lanes], grad.at[:, place], l_gu.at[s]).start()
            send(st_gu.at[s, theirs, lanes], grad.at[:, place], s_gg.at[s], r_gg.at[r], other)

    x, h = t // 2, t % 2

    def reduce_left(k, acc):
        drain(rx.at[k, 1], r_x.at[k, 1])
        for m in range(4):
            strip = at(x ^ ((m + 1) % 4), 2 * td)
            value = acc[strip, left] + rx[k, 1, strip, :]
            if m < 3:
                ta[k, m] = value.astype(BF)
                send(ta.at[k, m], ra.at[k, m], s_a.at[k], r_a.at[k], shard(2 * (m + 1)))
            else:
                rx[k, 1, strip, :] = value

    def reduce_right(k, acc):
        drain(rx.at[k, 0], r_x.at[k, 0])
        for m in range(4):
            place = at(m * 2 + 1 - h, td)
            tb[k, m] = (acc[place, right] + rx[k, 0, place, :]).astype(BF)
        send(tb.at[k], rb.at[k], s_b.at[k], r_b.at[k], shard(1))
        for m in range(4):
            place = at(m * 2 + h, td)
            rx[k, 0, place, :] = acc[place, right] + rx[k, 0, place, :]

    def reduce_cross(k):
        drain(rb.at[k], r_b.at[k])
        for m in range(4):
            over = x ^ ((m + 1) % 4)
            place = at(over * 2 + h, td)
            value = rx[k, 0, place, :] + rb[k, over].astype(F32)
            if m < 3:
                tc[k, m] = value.astype(BF)
                send(tc.at[k, m], rc.at[k, m], s_c.at[k], r_c.at[k], shard(2 * (m + 1)))
            else:
                rx[k, 0, place, :] = value
        drain(ra.at[k], r_a.at[k])
        for e in (1, 0):
            block = rx.at[k, 1, at(t ^ e, td)]
            total = block[...]
            for d in range(3):
                total = total + ra[k, d, at(h ^ e, td), :].astype(F32)
            block[...] = total
            if e == 1:
                send(block, ry.at[k], s_y.at[k], r_y.at[k], shard(1))

    def reduce_done(k, result):
        drain(rc.at[k], r_c.at[k])
        total = rx[k, 0, at(t, td), :]
        for d in range(3):
            total = total + rc[k, d].astype(F32)
        to[k, :, hd:] = total.astype(BF)
        drain(ry.at[k], r_y.at[k])
        to[k, :, :hd] = (rx[k, 1, at(t, td), :] + ry[k]).astype(BF)
        pltpu.make_async_copy(to.at[k], result, l_o.at[k]).start()
        drain(rx.at[k], s_x.at[k])
        drain(ta.at[k], s_a.at[k])
        drain(tb.at[k], s_b.at[k])
        drain(tc.at[k], s_c.at[k])
        drain(ry.at[k], s_y.at[k])

    use = LAG[5]

    def some(i, hop):
        for crossings, chosen in ((3, i % 4 == 1), (2, i % 4 != 1)):
            pl.when(chosen)(functools.partial(hop, d_all.at[i], sd_dl.at[i], rv_dl.at[i], crossings))

    def stage(v, lag, fwd, bwd):
        i = v - lag
        pl.when((i >= 0) & (i < nc))(lambda: fwd(i))
        pl.when((i >= nc) & (i < 2 * nc))(lambda: bwd(i))

    @pl.loop(0, 2 * nc + use)
    def _(v):
        stage(
            v, LAG[4],
            lambda i: gather_third(h_of(i), sd_h.at[i], rv_h.at[i], 3),
            lambda i: some(i - nc, gather_third),
        )
        stage(
            v, LAG[3],
            lambda i: gather_second(h_of(i), sd_h.at[i], rv_h.at[i], 3),
            lambda i: some(i - nc, gather_second),
        )
        stage(v, LAG[2], fwd_sum, bwd_sum)
        stage(v, 0, fwd_partial, bwd_partial)
        stage(v, LAG[2] + 1, lambda i: sum_sent(i, 2 * CW), lambda i: sum_sent(i, CW))
        stage(v, LAG[1], lambda i: sum_third(i, 2 * CW), lambda i: sum_third(i, CW))
        stage(v, LAG[0], lambda i: sum_second(i, 2 * CW), lambda i: sum_second(i, CW))

        @pl.when(v == use - 4)
        def _():
            forward_blocks(1, o_all)

        @pl.when(v == use)
        def _():
            await_blocks(1, o_all)
            drain(w_d.at[:, mine], ld_d)
            drain(w_d.at[:, theirs], rv_d)

        @pl.when((v >= nc) & (v < nc + nt))
        def _():
            x_t[:, at(v - nc, td)] = x_all[at(v - nc, td), :].T

        stage(v, use, fwd_use, lambda i: bwd_use(i - nc))

        @pl.when(v == nc + use)
        def _():
            reduce_right(0, out_acc)
            reduce_left(0, out_acc)

        @pl.when(v == nc + use + 4)
        def _():
            reduce_cross(0)

        @pl.when(v == nc + use + 7)
        def _():
            reduce_done(0, out)

    reduce_right(1, in_acc)
    reduce_left(1, in_acc)
    pl.loop(nc - sum(LATE), nc - LATE[1])(weight_grads)
    reduce_cross(1)
    pl.loop(nc - LATE[1], nc)(weight_grads)
    reduce_done(1, ig)

    for s in range(2):
        drain(st_d.at[s, :, mine], l_dg.at[s])
        drain(st_d.at[s, :, theirs], s_dg.at[s])
        drain(st_gu.at[s, mine], l_gu.at[s])
        drain(st_gu.at[s, theirs], s_gg.at[s])
        drain(to.at[s], l_o.at[s])
    partner = at(oc, fh)
    drain(dg.at[partner, :], r_dg)
    drain(gg.at[:, partner], r_gg.at[0])
    drain(ug.at[:, partner], r_gg.at[1])
    drain(w_gu.at[:, mine], sd_w)
    drain(w_d.at[:, mine], sd_d)
    for k, ref in enumerate((x_all, o_all)):
        drain(ref.at[:, pl.ds(0, dd)], sd_a.at[k])
        drain(ref.at[pl.ds(0, (nt - 1) * td), pl.ds(0, dd)], sf_a.at[k])


PIECES = 4


def hand_over(*refs):
    srcs, dsts, holds, (ins, outs) = refs[:5], refs[5:10], refs[10:15], refs[15:]
    pieces = []
    for j in (2, 3, 4, 0, 1):
        n = srcs[j].shape[0] // PIECES
        for p in range(PIECES):
            place = pl.ds(p * n, n)
            pieces.append((
                pltpu.make_async_copy(srcs[j].at[place], holds[j].at[place], ins.at[j, p]),
                pltpu.make_async_copy(holds[j].at[place], dsts[j].at[place], outs.at[j, p]),
            ))
    for copy, _ in pieces:
        copy.start()
    for copy, leave in pieces:
        copy.wait()
        leave.start()
    for _, leave in pieces:
        leave.wait()


def per_device(tokens, gate_weight, up_weight, down_weight, out_grad):
    nt = lax.axis_size("tensor")
    td, dd = tokens.shape
    ff = gate_weight.shape[1]
    fh = ff // 2
    nc = fh // CW
    n = nt * td
    tq = n // (2 * NZ)
    d2, hd = 2 * dd, dd // 2
    vmem = pltpu.VMEM
    dma = pltpu.SemaphoreType.DMA
    anywhere = pl.BlockSpec(memory_space=pl.ANY)
    results = pl.pallas_call(
        functools.partial(kernel, (nt, td, dd, tq, fh, nc)),
        name="swiglu",
        out_shape=(
            jax.ShapeDtypeStruct((td, dd), BF),
            jax.ShapeDtypeStruct((td, dd), BF),
            jax.ShapeDtypeStruct((dd, ff), BF),
            jax.ShapeDtypeStruct((dd, ff), BF),
            jax.ShapeDtypeStruct((ff, dd), BF),
        ),
        in_specs=[anywhere] * 5,
        out_specs=(anywhere,) * 5,
        scratch_shapes=[
            vmem((nc, d2, 2 * CW), BF),
            vmem((fh, d2), BF),
            vmem((n, d2), BF),
            vmem((d2, n), BF),
            vmem((n, d2), BF),
            vmem((nc // 2, n, 2 * CW), BF),
            vmem((nc, n, 2 * CW), BF),
            vmem((n, d2), F32),
            vmem((n, d2), F32),
            vmem((n, 2 * CW), F32),
            vmem((SLOTS, 5, tq, 2 * CW), F32),
            vmem((SLOTS, 3, tq, 2 * CW), BF),
            vmem((SLOTS, 2, tq, 2 * CW), BF),
            vmem((SLOTS, 2, tq, 2 * CW), BF),
            vmem((SLOTS, 3, tq, 2 * CW), BF),
            vmem((SLOTS, 2, tq, 2 * CW), BF),
            vmem((SLOTS, 2, tq, 2 * CW), BF),
            vmem((nc, tq, 2 * CW), F32),
            vmem((2, 2 * CW, d2), BF),
            vmem((2, d2, 2 * CW), BF),
            vmem((2, 2, n, hd), F32),
            vmem((2, td, hd), F32),
            vmem((2, 3, 2 * td, hd), BF),
            vmem((2, 3, 2 * td, hd), BF),
            vmem((2, 4, td, hd), BF),
            vmem((2, 4, td, hd), BF),
            vmem((2, 3, td, hd), BF),
            vmem((2, 3, td, hd), BF),
            vmem((2, td, dd), BF),
            dma((nc,)), dma((nc,)), dma,
            dma, dma, dma,
            dma((2,)), dma((2, nt, 2)), dma((2,)), dma((2, nt, 2)), dma((2,)),
            pltpu.SemaphoreType.REGULAR((3,)),
            dma((SLOTS,)), dma((SLOTS,)), dma((SLOTS,)),
            dma((SLOTS,)), dma((SLOTS,)), dma((SLOTS,)), dma((SLOTS,)),
            dma((nc,)), dma((nc, 3)), dma((nc,)), dma((nc, 3)),
            dma((2,)), dma((2,)), dma,
            dma((2,)), dma((2,)), dma((2,)),
            dma((2,)), dma((2, 2)), dma((2,)), dma((2,)), dma((2,)), dma((2,)), dma((2,)), dma((2,)), dma((2,)), dma((2,)), dma((2,)),
        ],
        compiler_params=pltpu.CompilerParams(
            collective_id=0, has_side_effects=True, vmem_limit_bytes=63 * 1024 * 1024
        ),
        cost_estimate=pl.CostEstimate(flops=18 * n * d2 * fh, bytes_accessed=6 * ff * dd * 2, transcendentals=0),
    )(tokens, gate_weight, up_weight, down_weight, out_grad)
    return pl.pallas_call(
        hand_over,
        name="hand_over",
        out_shape=tuple(jax.ShapeDtypeStruct(r.shape, r.dtype) for r in results),
        in_specs=[anywhere] * 5,
        out_specs=(anywhere,) * 5,
        scratch_shapes=[vmem(r.shape, r.dtype) for r in results] + [dma((5, PIECES)), dma((5, PIECES))],
        compiler_params=pltpu.CompilerParams(vmem_limit_bytes=60 * 1024 * 1024),
    )(*results)


def solution(mesh):
    act, wide, tall = P("tensor", "pipe"), P("pipe", "tensor"), P("tensor", "pipe")
    return jax.shard_map(
        per_device,
        mesh=mesh,
        in_specs=(act, wide, wide, tall, act),
        out_specs=(act, act, wide, wide, tall),
        check_vma=False,
    )
```

```python
import functools

import jax
import jax.numpy as jnp
from jax import lax
from jax.experimental import pallas as pl
from jax.experimental.pallas import tpu as pltpu
from jax.sharding import PartitionSpec as P

MESH = pl.DeviceIdType.MESH
BF = jnp.bfloat16
F32 = jnp.float32
NZ = 4
CW = 128
SOON = 2
SLOTS = 8
LAG = (2, 4, 6, 8, 10, 11)
LATE = (3, 2)


def dot_nn(a, b):
    return lax.dot_general(a, b, (((1,), (0,)), ((), ())), preferred_element_type=F32)


def dot_nt(a, b):
    return lax.dot_general(a, b, (((1,), (1,)), ((), ())), preferred_element_type=F32)


def dot_tn(a, b):
    return lax.dot_general(a, b, (((0,), (0,)), ((), ())), preferred_element_type=F32)


def drain(ref, sem):
    pltpu.make_async_copy(ref, ref, sem).wait()


def kernel(
    dims,
    tok, wg, wu, wd, og,
    out, ig, gg, ug, dg,
    w_gu, w_d, x_all, x_t, o_all, h_all, d_all, out_acc, in_acc, part,
    keep, s1, s2, s3, r1, r2, r3, gu, st_d, st_gu, rx, ry, ta, ra, tb, rb, tc, rc, to,
    ld_w, rv_w, sd_w, ld_d, rv_d, sd_d, ld_a, rv_a, sd_a, rf_a, sf_a,
    free, sd_1, sd_2, sd_3, rv_1, rv_2, rv_3, rv_4, sd_h, rv_h, sd_dl, rv_dl,
    l_dg, s_dg, r_dg, l_gu, s_gg, r_gg, s_x, r_x, s_a, r_a, s_b, r_b, s_c, r_c, s_y, r_y, l_o,
):
    nt, td, dd, tq, fh, nc = dims
    pipe, t = lax.axis_index("pipe"), lax.axis_index("tensor")
    q, c = pipe // 2, pipe % 2
    oc = 1 - c
    tokens = nt * td

    z, y = q // 2, q % 2

    def chip(dz, dy):
        return lax.rem(z + dz + NZ, NZ) * 2 + (y ^ dy)

    up_z, down_z, over_y = ((chip(dz, dy) * 2 + c, t) for dz, dy in ((1, 0), (-1, 0), (0, 1)))

    def shard(d):
        return (pipe, t ^ d)

    other = (q * 2 + oc, t)

    def send(src, dst, s, r, dev):
        pltpu.make_async_remote_copy(
            src_ref=src, dst_ref=dst, send_sem=s, recv_sem=r, device_id=dev, device_id_type=MESH
        ).start()

    def at(i, n):
        return pl.ds(pl.multiple_of(i * n, n), n)

    mine, theirs = at(c, dd), at(oc, dd)

    @pl.loop(0, nc)
    def _(i):
        cols = pl.ds(pl.multiple_of(c * fh + i * CW, CW), CW)
        for j, w in enumerate((wg, wu)):
            pltpu.make_async_copy(w.at[:, cols], w_gu.at[i, mine, pl.ds(j * CW, CW)], ld_w.at[i]).start()

    pltpu.make_async_copy(wd.at[at(c, fh), :], w_d.at[:, mine], ld_d).start()

    barrier = pltpu.get_barrier_semaphore()
    for near in (up_z, down_z, over_y):
        pl.semaphore_signal(barrier, inc=1, device_id=near, device_id_type=MESH)
    for d in (1, 2, 4, 6):
        pl.semaphore_signal(barrier, inc=1, device_id=shard(d), device_id_type=MESH)
    pl.semaphore_signal(barrier, inc=1, device_id=other, device_id_type=MESH)
    pl.semaphore_wait(barrier, 8)

    hd = dd // 2
    left = pl.ds(pl.multiple_of(c * dd, hd), hd)
    right = pl.ds(pl.multiple_of(c * dd + hd, hd), hd)

    def spread(k, src, dst):
        place = at(t, td)
        for d, first in ((2, False), (4, False), (6, False), (1, True), (2, True), (4, True), (6, True), (1, False)):
            cols, j = (left, 0) if first else (right, 1)
            send(src.at[:, pl.ds(j * hd, hd)], dst.at[place, cols], sd_a.at[k], rv_a.at[k, d, j], shard(d))
        block = dst.at[place, mine]
        pltpu.make_async_copy(src, block, ld_a.at[k]).start()
        send(src, block, sd_a.at[k], rf_a.at[k, 0, 0], other)

    spread(0, tok, x_all)

    def give_weights(i):
        cols = pl.ds(pl.multiple_of(oc * fh + i * CW, CW), CW)
        for j, w in enumerate((wg, wu)):
            send(w.at[:, cols], w_gu.at[i, mine, pl.ds(j * CW, CW)], sd_w, rv_w.at[i], other)

    pl.loop(0, SOON)(give_weights)

    def forward_blocks(k, ref):
        order = [(1, 0), (2, 1), (4, 1), (6, 1), (2, 0), (4, 0), (6, 0), (1, 1)]
        order += [(3, 0), (3, 1), (5, 0), (5, 1), (7, 0), (7, 1)]
        for d, j in order:
            block = ref.at[at(t ^ d, td), (left, right)[j]]
            drain(block, rv_a.at[k, d, j])
            if d == 1 and (j == 0 or k == 1):
                for e in (2, 4, 6):
                    send(block, block, sd_a.at[k], rv_a.at[k, e + 1, j], shard(e))
            elif d in (2, 4, 6) and j == 1 and k == 0:
                send(block, block, sd_a.at[k], rv_a.at[k, d + 1, j], shard(1))
            send(block, block, sf_a.at[k], rf_a.at[k, d, j], other)

    def await_blocks(k, ref):
        drain(ref.at[at(t, td), mine], ld_a.at[k])
        drain(ref.at[at(t, td), theirs], rf_a.at[k, 0, 0])
        for d in range(1, nt):
            for j in range(2):
                cols = pl.ds(pl.multiple_of(oc * dd + j * hd, hd), hd)
                drain(ref.at[at(t ^ d, td), cols], rf_a.at[k, d, j])

    forward_blocks(0, x_all)
    spread(1, og, o_all)
    pl.loop(SOON, nc)(give_weights)
    send(wd.at[at(oc, fh), :], w_d.at[:, mine], sd_d, rv_d, other)
    await_blocks(0, x_all)

    half = tokens // 2

    hq = tq // 2
    low, high = pl.ds(0, hq), pl.ds(hq, hq)

    def sum_first(v, width):
        slot, w = lax.rem(v, SLOTS), pl.ds(0, width)

        @pl.when(v >= SLOTS)
        def _():
            for j in range(3):
                pl.semaphore_wait(free.at[j], 1)

        for j, (dz, dy) in enumerate(((0, 0), (1, 0), (-1, 0), (2, 0), (0, 1))):
            keep[slot, j, :, w] = part[at(chip(dz, dy), tq), w]
        for j, (dz, dev) in enumerate(((2, over_y), (1, up_z), (-1, down_z))):
            s1[slot, j, :, w] = part[at(chip(dz, 1), tq), w].astype(BF)
            send(s1.at[slot, j, :, w], r1.at[slot, j, :, w], sd_1.at[slot], rv_1.at[slot], dev)

    def sum_second(v, width):
        slot, w = lax.rem(v, SLOTS), pl.ds(0, width)
        drain(r1.at[slot, :, :, w], rv_1.at[slot])
        s2[slot, 0, :, w] = (keep[slot, 3, :, w] + r1[slot, 0, :, w].astype(F32)).astype(BF)
        s2[slot, 1, :, w] = (
            keep[slot, 4, :, w] + r1[slot, 1, :, w].astype(F32) + r1[slot, 2, :, w].astype(F32)
        ).astype(BF)
        for rows, dev in ((low, down_z), (high, up_z)):
            send(s2.at[slot, 0, rows, w], r2.at[slot, 0, rows, w], sd_2.at[slot], rv_2.at[slot], dev)
        send(s2.at[slot, 1, :, w], r2.at[slot, 1, :, w], sd_2.at[slot], rv_3.at[slot], over_y)

    def sum_third(v, width):
        slot, w = lax.rem(v, SLOTS), pl.ds(0, width)
        drain(r2.at[slot, 0, :, w], rv_2.at[slot])
        s3[slot, 0, low, w] = (keep[slot, 2, low, w] + r2[slot, 0, low, w].astype(F32)).astype(BF)
        s3[slot, 0, high, w] = keep[slot, 2, high, w].astype(BF)
        s3[slot, 1, low, w] = keep[slot, 1, low, w].astype(BF)
        s3[slot, 1, high, w] = (keep[slot, 1, high, w] + r2[slot, 0, high, w].astype(F32)).astype(BF)
        for j, dev in enumerate((down_z, up_z)):
            send(s3.at[slot, j, :, w], r3.at[slot, j, :, w], sd_3.at[slot], rv_4.at[slot], dev)

    def sum_total(v, width):
        slot, w = lax.rem(v, SLOTS), pl.ds(0, width)
        drain(r2.at[slot, 1, :, w], rv_3.at[slot])
        drain(r3.at[slot, :, :, w], rv_4.at[slot])
        total = (keep[slot, 0, :, w] + r2[slot, 1, :, w].astype(F32)) + (
            r3[slot, 0, :, w].astype(F32) + r3[slot, 1, :, w].astype(F32)
        )

        @pl.when(v < 2 * nc - SLOTS)
        def _():
            for j, dev in enumerate((down_z, up_z, over_y)):
                pl.semaphore_signal(free.at[j], inc=1, device_id=dev, device_id_type=MESH)

        return total

    def sum_sent(v, width):
        slot, w = lax.rem(v, SLOTS), pl.ds(0, width)
        drain(s1.at[slot, :, :, w], sd_1.at[slot])
        drain(s2.at[slot, :, :, w], sd_2.at[slot])
        drain(s3.at[slot, :, :, w], sd_3.at[slot])

    def gather_first(ref, sd, rv):
        block = ref.at[at(q, tq)]
        for dev in (up_z, down_z, over_y):
            send(block, block, sd, rv.at[0], dev)

    def gather_second(ref, sd, rv, crossings):
        drain(ref.at[pl.ds(0, 3 * tq)], rv.at[0])
        below, above, beside = (chip(dz, dy) * tq for dz, dy in ((-1, 0), (1, 0), (0, 1)))
        moves = [(below, hq, up_z), (above + hq, hq, down_z)]
        if crossings == 3:
            moves += [(below, tq, over_y), (above, tq, over_y)]
        else:
            moves += [(beside, tq, up_z), (beside, tq, down_z)]
        for first, n, dev in moves:
            block = ref.at[pl.ds(pl.multiple_of(first, hq), n)]
            send(block, block, sd, rv.at[1], dev)

    def gather_third(ref, sd, rv, crossings):
        drain(ref.at[pl.ds(0, 3 * tq)], rv.at[1])
        if crossings == 3:
            moves = [(chip(-1, 1) * tq, hq, up_z), (chip(1, 1) * tq + hq, hq, down_z)]
        else:
            moves = [(chip(2, 0) * tq, tq, over_y)]
        for first, n, dev in moves:
            block = ref.at[pl.ds(pl.multiple_of(first, hq), n)]
            send(block, block, sd, rv.at[2], dev)

    def gather_done(ref, sd, rv):
        drain(ref.at[pl.ds(0, tq)], rv.at[2])
        drain(ref.at[pl.ds(0, 7 * tq)], sd)

    def col_block(m):
        return pl.ds(pl.multiple_of(((oc * 2 + 1 - m % 2 + m // 2 * 2) % 4) * hd, hd), hd)

    def h_of(i):
        return h_all.at[i // 2, :, at(i % 2, CW)]

    def fwd_partial(v):
        drain(w_gu.at[v, mine], ld_w.at[v])
        drain(w_gu.at[v, theirs], rv_w.at[v])

        @pl.loop(0, 2)
        def _(m):
            part[at(m, half), :] = dot_nn(x_all[at(m, half), :], w_gu[v])

        sum_first(v, 2 * CW)

    def fwd_sum(v):
        total = sum_total(v, 2 * CW)
        gu[v] = total
        gate, up = total[:, :CW], total[:, CW:]
        block = h_of(v).at[at(q, tq)]
        block[...] = (gate * jax.nn.sigmoid(gate) * up).astype(BF)
        gather_first(h_of(v), sd_h.at[v], rv_h.at[v])

    def fwd_use(i):
        gather_done(h_of(i), sd_h.at[i], rv_h.at[i])
        pl.when(i % 2 == 1)(lambda: fwd_pair(i // 2))

    def fwd_pair(p):
        @pl.loop(0, 4)
        def _(m):
            cols = col_block(m)
            value = dot_nn(h_all[p], w_d[at(p, 2 * CW), cols])

            @pl.when(p == 0)
            def _():
                out_acc[:, cols] = value

            @pl.when(p > 0)
            def _():
                out_acc[:, cols] += value

            @pl.when((p == nc // 2 - 1) & (m < 2))
            def _():
                send(out_acc.at[:, cols], rx.at[0, m], s_x.at[0], r_x.at[0, m], other)

        s = lax.rem(p, 2)
        place = pl.ds(pl.multiple_of(c * fh + p * (2 * CW), CW), 2 * CW)

        @pl.when(p >= 2)
        def _():
            drain(st_d.at[s, :, mine], l_dg.at[s])
            drain(st_d.at[s, :, theirs], s_dg.at[s])

        st_d[s] = dot_tn(h_all[p], o_all[...]).astype(BF)
        pltpu.make_async_copy(st_d.at[s, :, mine], dg.at[place, :], l_dg.at[s]).start()
        send(st_d.at[s, :, theirs], dg.at[place, :], s_dg.at[s], r_dg, other)

    def bwd_partial(v):
        @pl.loop(0, 2)
        def _(m):
            part[at(m, half), pl.ds(0, CW)] = dot_nt(o_all[at(m, half), :], w_d[at(v - nc, CW), :])

        sum_first(v, CW)

    def bwd_sum(v):
        total = sum_total(v, CW)
        i = v - nc
        gate, up = gu[i, :, :CW], gu[i, :, CW:]
        sigma = jax.nn.sigmoid(gate)
        d_all[i, at(q, tq), :CW] = (total * up * sigma * (1.0 + gate * (1.0 - sigma))).astype(BF)
        d_all[i, at(q, tq), CW:] = (total * (gate * sigma)).astype(BF)
        gather_first(d_all.at[i], sd_dl.at[i], rv_dl.at[i])

    def bwd_use(i):
        gather_done(d_all.at[i], sd_dl.at[i], rv_dl.at[i])

        @pl.loop(0, 4)
        def _(m):
            cols = col_block(m)
            value = dot_nt(d_all[i], w_gu[i, cols, :])

            @pl.when(i == 0)
            def _():
                in_acc[:, cols] = value

            @pl.when(i > 0)
            def _():
                in_acc[:, cols] += value

            @pl.when((i == nc - 1) & (m < 2))
            def _():
                send(in_acc.at[:, cols], rx.at[1, m], s_x.at[1], r_x.at[1, m], other)

        pl.when(i < nc - sum(LATE))(lambda: weight_grads(i))

    def weight_grads(i):
        s = lax.rem(i, 2)
        place = pl.ds(pl.multiple_of(c * fh + i * CW, CW), CW)

        @pl.when(i >= 2)
        def _():
            drain(st_gu.at[s, mine], l_gu.at[s])
            drain(st_gu.at[s, theirs], s_gg.at[s])

        @pl.loop(0, 2)
        def _(m):
            st_gu[s, at(m, dd), :] = dot_nn(x_t[at(m, dd), :], d_all[i]).astype(BF)

        for j, (grad, r) in enumerate(((gg, 0), (ug, 1))):
            lanes = pl.ds(j * CW, CW)
            pltpu.make_async_copy(st_gu.at[s, mine, lanes], grad.at[:, place], l_gu.at[s]).start()
            send(st_gu.at[s, theirs, lanes], grad.at[:, place], s_gg.at[s], r_gg.at[r], other)

    x, h = t // 2, t % 2

    def reduce_left(k, acc):
        drain(rx.at[k, 1], r_x.at[k, 1])
        for m in range(4):
            strip = at(x ^ ((m + 1) % 4), 2 * td)
            value = acc[strip, left] + rx[k, 1, strip, :]
            if m < 3:
                ta[k, m] = value.astype(BF)
                send(ta.at[k, m], ra.at[k, m], s_a.at[k], r_a.at[k], shard(2 * (m + 1)))
            else:
                rx[k, 1, strip, :] = value

    def reduce_right(k, acc):
        drain(rx.at[k, 0], r_x.at[k, 0])
        for m in range(4):
            place = at(m * 2 + 1 - h, td)
            tb[k, m] = (acc[place, right] + rx[k, 0, place, :]).astype(BF)
        send(tb.at[k], rb.at[k], s_b.at[k], r_b.at[k], shard(1))
        for m in range(4):
            place = at(m * 2 + h, td)
            rx[k, 0, place, :] = acc[place, right] + rx[k, 0, place, :]

    def reduce_cross(k):
        drain(rb.at[k], r_b.at[k])
        for m in range(4):
            over = x ^ ((m + 1) % 4)
            place = at(over * 2 + h, td)
            value = rx[k, 0, place, :] + rb[k, over].astype(F32)
            if m < 3:
                tc[k, m] = value.astype(BF)
                send(tc.at[k, m], rc.at[k, m], s_c.at[k], r_c.at[k], shard(2 * (m + 1)))
            else:
                rx[k, 0, place, :] = value
        drain(ra.at[k], r_a.at[k])
        for e in (1, 0):
            block = rx.at[k, 1, at(t ^ e, td)]
            total = block[...]
            for d in range(3):
                total = total + ra[k, d, at(h ^ e, td), :].astype(F32)
            block[...] = total
            if e == 1:
                send(block, ry.at[k], s_y.at[k], r_y.at[k], shard(1))

    def reduce_done(k, result):
        drain(rc.at[k], r_c.at[k])
        total = rx[k, 0, at(t, td), :]
        for d in range(3):
            total = total + rc[k, d].astype(F32)
        to[k, :, hd:] = total.astype(BF)
        drain(ry.at[k], r_y.at[k])
        to[k, :, :hd] = (rx[k, 1, at(t, td), :] + ry[k]).astype(BF)
        pltpu.make_async_copy(to.at[k], result, l_o.at[k]).start()
        drain(rx.at[k], s_x.at[k])
        drain(ta.at[k], s_a.at[k])
        drain(tb.at[k], s_b.at[k])
        drain(tc.at[k], s_c.at[k])
        drain(ry.at[k], s_y.at[k])

    use = LAG[5]

    def some(i, hop):
        for crossings, chosen in ((3, i % 4 == 1), (2, i % 4 != 1)):
            pl.when(chosen)(functools.partial(hop, d_all.at[i], sd_dl.at[i], rv_dl.at[i], crossings))

    def stage(v, lag, fwd, bwd):
        i = v - lag
        pl.when((i >= 0) & (i < nc))(lambda: fwd(i))
        pl.when((i >= nc) & (i < 2 * nc))(lambda: bwd(i))

    @pl.loop(0, 2 * nc + use)
    def _(v):
        stage(
            v, LAG[4],
            lambda i: gather_third(h_of(i), sd_h.at[i], rv_h.at[i], 3),
            lambda i: some(i - nc, gather_third),
        )
        stage(
            v, LAG[3],
            lambda i: gather_second(h_of(i), sd_h.at[i], rv_h.at[i], 3),
            lambda i: some(i - nc, gather_second),
        )
        stage(v, LAG[2], fwd_sum, bwd_sum)
        stage(v, 0, fwd_partial, bwd_partial)
        stage(v, LAG[2] + 1, lambda i: sum_sent(i, 2 * CW), lambda i: sum_sent(i, CW))
        stage(v, LAG[1], lambda i: sum_third(i, 2 * CW), lambda i: sum_third(i, CW))
        stage(v, LAG[0], lambda i: sum_second(i, 2 * CW), lambda i: sum_second(i, CW))

        @pl.when(v == use - 4)
        def _():
            forward_blocks(1, o_all)

        @pl.when(v == use)
        def _():
            await_blocks(1, o_all)
            drain(w_d.at[:, mine], ld_d)
            drain(w_d.at[:, theirs], rv_d)

        @pl.when((v >= nc) & (v < nc + nt))
        def _():
            x_t[:, at(v - nc, td)] = x_all[at(v - nc, td), :].T

        stage(v, use, fwd_use, lambda i: bwd_use(i - nc))

        @pl.when(v == nc + use)
        def _():
            reduce_right(0, out_acc)
            reduce_left(0, out_acc)

        @pl.when(v == nc + use + 4)
        def _():
            reduce_cross(0)

        @pl.when(v == nc + use + 7)
        def _():
            reduce_done(0, out)

    reduce_right(1, in_acc)
    reduce_left(1, in_acc)
    pl.loop(nc - sum(LATE), nc - LATE[1])(weight_grads)
    reduce_cross(1)
    pl.loop(nc - LATE[1], nc)(weight_grads)
    reduce_done(1, ig)

    for s in range(2):
        drain(st_d.at[s, :, mine], l_dg.at[s])
        drain(st_d.at[s, :, theirs], s_dg.at[s])
        drain(st_gu.at[s, mine], l_gu.at[s])
        drain(st_gu.at[s, theirs], s_gg.at[s])
        drain(to.at[s], l_o.at[s])
    partner = at(oc, fh)
    drain(dg.at[partner, :], r_dg)
    drain(gg.at[:, partner], r_gg.at[0])
    drain(ug.at[:, partner], r_gg.at[1])
    drain(w_gu.at[:, mine], sd_w)
    drain(w_d.at[:, mine], sd_d)
    for k, ref in enumerate((x_all, o_all)):
        drain(ref.at[:, pl.ds(0, dd)], sd_a.at[k])
        drain(ref.at[pl.ds(0, (nt - 1) * td), pl.ds(0, dd)], sf_a.at[k])


PIECES = 4


def hand_over(*refs):
    srcs, dsts, holds, (ins, outs) = refs[:5], refs[5:10], refs[10:15], refs[15:]
    pieces = []
    for j in (2, 3, 4, 0, 1):
        n = srcs[j].shape[0] // PIECES
        for p in range(PIECES):
            place = pl.ds(p * n, n)
            pieces.append((
                pltpu.make_async_copy(srcs[j].at[place], holds[j].at[place], ins.at[j, p]),
                pltpu.make_async_copy(holds[j].at[place], dsts[j].at[place], outs.at[j, p]),
            ))
    for copy, _ in pieces:
        copy.start()
    for copy, leave in pieces:
        copy.wait()
        leave.start()
    for _, leave in pieces:
        leave.wait()


def per_device(tokens, gate_weight, up_weight, down_weight, out_grad):
    nt = lax.axis_size("tensor")
    td, dd = tokens.shape
    ff = gate_weight.shape[1]
    fh = ff // 2
    nc = fh // CW
    n = nt * td
    tq = n // (2 * NZ)
    d2, hd = 2 * dd, dd // 2
    vmem = pltpu.VMEM
    dma = pltpu.SemaphoreType.DMA
    anywhere = pl.BlockSpec(memory_space=pl.ANY)
    results = pl.pallas_call(
        functools.partial(kernel, (nt, td, dd, tq, fh, nc)),
        name="swiglu",
        out_shape=(
            jax.ShapeDtypeStruct((td, dd), BF),
            jax.ShapeDtypeStruct((td, dd), BF),
            jax.ShapeDtypeStruct((dd, ff), BF),
            jax.ShapeDtypeStruct((dd, ff), BF),
            jax.ShapeDtypeStruct((ff, dd), BF),
        ),
        in_specs=[anywhere] * 5,
        out_specs=(anywhere,) * 5,
        scratch_shapes=[
            vmem((nc, d2, 2 * CW), BF),
            vmem((fh, d2), BF),
            vmem((n, d2), BF),
            vmem((d2, n), BF),
            vmem((n, d2), BF),
            vmem((nc // 2, n, 2 * CW), BF),
            vmem((nc, n, 2 * CW), BF),
            vmem((n, d2), F32),
            vmem((n, d2), F32),
            vmem((n, 2 * CW), F32),
            vmem((SLOTS, 5, tq, 2 * CW), F32),
            vmem((SLOTS, 3, tq, 2 * CW), BF),
            vmem((SLOTS, 2, tq, 2 * CW), BF),
            vmem((SLOTS, 2, tq, 2 * CW), BF),
            vmem((SLOTS, 3, tq, 2 * CW), BF),
            vmem((SLOTS, 2, tq, 2 * CW), BF),
            vmem((SLOTS, 2, tq, 2 * CW), BF),
            vmem((nc, tq, 2 * CW), F32),
            vmem((2, 2 * CW, d2), BF),
            vmem((2, d2, 2 * CW), BF),
            vmem((2, 2, n, hd), F32),
            vmem((2, td, hd), F32),
            vmem((2, 3, 2 * td, hd), BF),
            vmem((2, 3, 2 * td, hd), BF),
            vmem((2, 4, td, hd), BF),
            vmem((2, 4, td, hd), BF),
            vmem((2, 3, td, hd), BF),
            vmem((2, 3, td, hd), BF),
            vmem((2, td, dd), BF),
            dma((nc,)), dma((nc,)), dma,
            dma, dma, dma,
            dma((2,)), dma((2, nt, 2)), dma((2,)), dma((2, nt, 2)), dma((2,)),
            pltpu.SemaphoreType.REGULAR((3,)),
            dma((SLOTS,)), dma((SLOTS,)), dma((SLOTS,)),
            dma((SLOTS,)), dma((SLOTS,)), dma((SLOTS,)), dma((SLOTS,)),
            dma((nc,)), dma((nc, 3)), dma((nc,)), dma((nc, 3)),
            dma((2,)), dma((2,)), dma,
            dma((2,)), dma((2,)), dma((2,)),
            dma((2,)), dma((2, 2)), dma((2,)), dma((2,)), dma((2,)), dma((2,)), dma((2,)), dma((2,)), dma((2,)), dma((2,)), dma((2,)),
        ],
        compiler_params=pltpu.CompilerParams(
            collective_id=0, has_side_effects=True, vmem_limit_bytes=63 * 1024 * 1024
        ),
        cost_estimate=pl.CostEstimate(flops=18 * n * d2 * fh, bytes_accessed=6 * ff * dd * 2, transcendentals=0),
    )(tokens, gate_weight, up_weight, down_weight, out_grad)
    return pl.pallas_call(
        hand_over,
        name="hand_over",
        out_shape=tuple(jax.ShapeDtypeStruct(r.shape, r.dtype) for r in results),
        in_specs=[anywhere] * 5,
        out_specs=(anywhere,) * 5,
        scratch_shapes=[vmem(r.shape, r.dtype) for r in results] + [dma((5, PIECES)), dma((5, PIECES))],
        compiler_params=pltpu.CompilerParams(vmem_limit_bytes=60 * 1024 * 1024),
    )(*results)


def solution(mesh):
    act, wide, tall = P("tensor", "pipe"), P("pipe", "tensor"), P("tensor", "pipe")
    return jax.shard_map(
        per_device,
        mesh=mesh,
        in_specs=(act, wide, wide, tall, act),
        out_specs=(act, act, wide, wide, tall),
        check_vma=False,
    )
```
